32 devices in a mesh: seq: 4 (over z), batch: 4 (over y, x), head: 2 (over core).
Axes of the slice: x: 2, y: 2, z: 4, core: 2. Of those that a mesh axis runs over, the one named last changes fastest.
Arguments:
- tokens: bfloat16 [4, 2048, 2048], P('batch', 'seq'), may hold values from -6 to 6
- prescale: float32 [2048], replicated, may hold values from 0.25 to 1.75
- query_weight: bfloat16 [2048, 2048], P('seq', 'head'), may hold values from -0.125 to 0.125
- key_weight: bfloat16 [2048, 2048], P('seq', 'head'), may hold values from -0.125 to 0.125
- value_weight: bfloat16 [2048, 4096], P('seq', 'head'), may hold values from -0.125 to 0.125
- gate_weight: bfloat16 [2048, 4096], P('seq', 'head'), may hold values from -0.125 to 0.125
- groupscale: float32 [4096], P('head'), may hold values from 0.25 to 1.75
- groupshift: float32 [4096], P('head'), may hold values from -3 to 3
- output_weight: bfloat16 [4096, 2048], P('head', 'seq'), may hold values from -0.09375 to 0.09375
- postscale: float32 [2048], replicated, may hold values from 0.25 to 1.75
- postshift: float32 [2048], replicated, may hold values from -3 to 3
- expand_weight: bfloat16 [2048, 4096], P('seq', 'head'), may hold values from -0.125 to 0.125
- hiddenbias: float32 [4096], P('head'), may hold values from -3 to 3
- reduce_weight: bfloat16 [4096, 2048], P('head', 'seq'), may hold values from -0.09375 to 0.09375
- outputbias: float32 [2048], replicated, may hold values from -3 to 3
- cotangent: bfloat16 [4, 2048, 2048], P('batch', 'seq'), may hold values from -6 to 6
- doc_lengths: int32 [4, 8], P('batch'), may hold values from 1 to 512, 2048 in all within a row
- segments: int32 [4, 2048], P('batch', 'seq'), may hold values from 0 to 2, as said below
Outputs:
- layer_output: bfloat16 [4, 2048, 2048], P('batch', 'seq')
- tokens_grad: float32 [4, 2048, 2048], P('batch', 'seq')
- prescale_grad: float32 [2048], replicated
- query_grad: float32 [2048, 2048], P('seq', 'head')
- key_grad: float32 [2048, 2048], P('seq', 'head')
- value_grad: float32 [2048, 4096], P('seq', 'head')
- gate_grad: float32 [2048, 4096], P('seq', 'head')
- groupscale_grad: float32 [4096], P('head')
- groupshift_grad: float32 [4096], P('head')
- output_grad: float32 [4096, 2048], P('head', 'seq')
- postscale_grad: float32 [2048], replicated
- postshift_grad: float32 [2048], replicated
- expand_grad: float32 [2048, 4096], P('seq', 'head')
- hiddenbias_grad: float32 [4096], P('head')
- reduce_grad: float32 [4096, 2048], P('head', 'seq')
- outputbias_grad: float32 [2048], replicated
The draws below stay inside these ranges and needn't reach their ends.
Inputs may be any that keep to these rules, and one draw needn't show every extreme that they name: segments are non-decreasing along each stream, 0 at its first token and 2 at its last; the id rises by one or more at each reset.
All inputs are finite; a program needn't handle non-finite values.
Results may differ from the reference program's by a relative error of at most 0.019.
Values may be sent and summed in bfloat16 or wider, within the bound.
No kernel may reach another device: no remote copies, remote signals or barrier semaphores. Data moves between devices by JAX's collectives and lax.ppermute only.
A program may use at most 384 MiB of HBM per device.

```python
import math
import jax
import jax.numpy as jnp
import numpy as np
from jax import lax

D = 2048
HEADS = 8
HV = 4096
FF = 4096
KEY = 256
VAL = 512
TOK_DEV = 512
DOCS = 8
RESETS = 2
STREAMS = 4
STREAM = 2048
DOC_MAX = 512


def draw_segments(key, part):
    key = jax.random.fold_in(key, 11)
    reset_points = jax.random.randint(key, (STREAMS, RESETS), 1, STREAM, dtype=jnp.int32)
    indices = jnp.arange(STREAM, dtype=jnp.int32)
    crossed = (indices[None, :, None] >= reset_points[:, None, :]).astype(jnp.int32)
    return jnp.sum(crossed, axis=-1).astype(jnp.int32)


def level_of(own_key, dims, split, low, top_value):
    loudness = 1.0
    for position, blocks in split:
        draws = jax.random.uniform(jax.random.fold_in(jax.random.fold_in(own_key, 6), position), (blocks,), jnp.float32, low / len(split), top_value / len(split))
        loudness = loudness * jnp.repeat(jnp.exp(draws), dims[position] // blocks).reshape((-1,) + (1,) * (len(dims) - 1 - position))
    return loudness


def profile(count, total, bound, slope):
    loads = [(1 << 20) // math.isqrt(rank ** slope) + 1 for rank in range(2, count + 1)]
    spare, counts = total - bound - (count - 1), [1] * (count - 1)
    while spare > 0:
        movable = [i for i in range(count - 1) if counts[i] < bound]
        mass, budget = sum([loads[i] for i in movable]), spare
        for i in movable:
            extra = min(bound - counts[i], max(1, budget * loads[i] // mass), spare)
            counts[i] = counts[i] + extra
            spare = spare - extra
    return np.array([bound] + counts)


def ragged(rng, amount, total, most, skew):
    if amount == 2:
        one = jax.random.randint(rng, (), max(1, total - most), min(most, total - 1) + 1)
        return jnp.stack([one, total - one])
    sizes = jnp.asarray(profile(amount, total, most, skew), jnp.int32)
    pairs = (amount - 1) // 2
    giver, sink = sizes[1:1 + 2 * pairs:2], sizes[2:2 + 2 * pairs:2]
    room = jnp.minimum(giver - 1, most - sink)
    moved = jax.random.randint(jax.random.fold_in(rng, 1), (pairs,), 0, 1 << 20) % (room + 1)
    sizes = sizes.at[1:1 + 2 * pairs:2].set(giver - moved).at[2:2 + 2 * pairs:2].set(sink + moved)
    return sizes[jax.random.permutation(jax.random.fold_in(rng, 2), amount)]


def scatter_about(key, shape, deviation, bound, cuts=(), kind=jnp.bfloat16):
    factor_of = level_of(key, shape, cuts, -0.22, 0.18) if cuts else 1.0
    drawn = jax.random.normal(key, shape, jnp.float32) * deviation * factor_of
    return jnp.minimum(jnp.maximum(drawn, -bound), bound).astype(kind)


def setup_inputs(seed: int = 0) -> dict:
    streams_of = jax.random.split(jax.random.key(seed), 19)
    return {
        "tokens": scatter_about(streams_of[0], (STREAMS, STREAM, D), 1.0, 6.0, ((0, 4), (1, 4))),
        "prescale": jnp.clip(1.0 + 0.15 * jax.random.normal(streams_of[1], (D,), jnp.float32), 0.25, 1.75),
        "query_weight": scatter_about(streams_of[2], (D, D), D ** -0.5, 0.125, ((0, 4), (1, 2))),
        "key_weight": scatter_about(streams_of[3], (D, D), D ** -0.5, 0.125, ((0, 4), (1, 2))),
        "value_weight": scatter_about(streams_of[4], (D, HV), D ** -0.5, 0.125, ((0, 4), (1, 2))),
        "gate_weight": scatter_about(streams_of[5], (D, HV), D ** -0.5, 0.125, ((0, 4), (1, 2))),
        "groupscale": jnp.clip(1.0 + 0.15 * jax.random.normal(streams_of[6], (HV,), jnp.float32), 0.25, 1.75),
        "groupshift": scatter_about(streams_of[7], (HV,), 0.5, 3.0, ((0, 2),), jnp.float32),
        "output_weight": scatter_about(streams_of[8], (HV, D), HV ** -0.5, 0.09375, ((0, 2), (1, 4))),
        "postscale": jnp.clip(1.0 + 0.15 * jax.random.normal(streams_of[9], (D,), jnp.float32), 0.25, 1.75),
        "postshift": scatter_about(streams_of[10], (D,), 0.5, 3.0, (), jnp.float32),
        "expand_weight": scatter_about(streams_of[11], (D, FF), D ** -0.5, 0.125, ((0, 4), (1, 2))),
        "hiddenbias": scatter_about(streams_of[12], (FF,), 0.5, 3.0, ((0, 2),), jnp.float32),
        "reduce_weight": scatter_about(streams_of[13], (FF, D), FF ** -0.5, 0.09375, ((0, 2), (1, 4))),
        "outputbias": scatter_about(streams_of[14], (D,), 0.5, 3.0, (), jnp.float32),
        "cotangent": scatter_about(streams_of[15], (STREAMS, STREAM, D), 1.0, 6.0, ((0, 4), (1, 4))),
        "doc_lengths": jax.vmap(lambda own: ragged(own, DOCS, STREAM, DOC_MAX, 2))(jax.random.split(streams_of[16], STREAMS)).reshape((STREAMS, DOCS)).astype(jnp.int32),
        "segments": draw_segments(jax.random.fold_in(streams_of[18], 71), 0),
    }


MAXIMUM_ACCURACY = lax.Precision.HIGHEST

@jax.custom_vjp
def low(v):
    return lax.optimization_barrier(v.astype(jnp.bfloat16)).astype(jnp.float32)

@jax.custom_vjp
def low_back(v):
    return v

def low_keep(v):
    return (low(v), None)

def low_pass(kept, grad):
    return (grad,)

def back_keep(v):
    return (v, None)

def back_low(kept, grad):
    return (low(grad),)
low.defvjp(low_keep, low_pass)
low_back.defvjp(back_keep, back_low)

def decay_logs(number, offset):
    heads_at = (offset + jnp.arange(number, dtype=jnp.int32)).astype(jnp.float32)
    return jnp.log1p(-jnp.exp2(-5.0 - heads_at))

def doc_positions(lengths, offset, number):
    lengths = lengths.astype(jnp.int32)
    doc_ends = jnp.cumsum(lengths).astype(jnp.int32)
    indices = (offset + jnp.arange(number, dtype=jnp.int32)).astype(jnp.int32)
    passed = jnp.where(doc_ends[None, :] <= indices[:, None], lengths[None, :], 0).astype(jnp.int32)
    doc_starts = lax.optimization_barrier(jnp.sum(passed, axis=1)).astype(jnp.int32)
    return (indices - doc_starts).astype(jnp.float32)

def rotation_tables(positions, key_size):
    middle = key_size // 2
    frequency = jnp.exp(-math.log(10000.0) * jnp.arange(middle, dtype=jnp.float32) / (middle - 1))
    phases = positions[..., None] * frequency
    return (jnp.cos(phases), jnp.sin(phases))

def rotate(values, cosine_table, sine_table):
    middle = values.shape[-1] // 2
    former, latter = (values[..., :middle], values[..., middle:])
    return jnp.concatenate([former * cosine_table - latter * sine_table, latter * cosine_table + former * sine_table], axis=-1)

def retention(queries, keys_in, values, segments, log_rates, block_size):
    segments = segments.astype(jnp.int32)
    length, head_count, key_size = queries.shape
    value_size = values.shape[-1]
    blocks = length // block_size
    indices = jnp.arange(block_size, dtype=jnp.int32)
    distance = (indices[:, None] - indices[None, :]).astype(jnp.int32)
    causal = distance >= 0
    decays = jnp.exp(jnp.where(causal, distance, 0).astype(jnp.float32)[None] * log_rates[:, None, None])
    entry_rate = jnp.exp((indices + 1).astype(jnp.float32)[None, :] * log_rates[:, None])
    exit_rate = jnp.exp((block_size - 1 - indices).astype(jnp.float32)[None, :] * log_rates[:, None])
    whole_rate = jnp.exp(block_size * log_rates)

    @jax.checkpoint
    def block_step(carry_in, pieces):
        retention_state, before = carry_in
        query_block, key_block, value_tile_rows, segment_block = pieces
        last_segment = segment_block[block_size - 1].astype(jnp.int32)
        linked = (segment_block[:, None] == segment_block[None, :]) & causal
        weights = jnp.where(linked[None], decays, 0.0)
        scores = low_back(jnp.einsum('nhk,mhk->hnm', query_block, key_block, precision=MAXIMUM_ACCURACY))
        mixing = low(scores * weights)
        entry_weight = entry_rate * (segment_block == before).astype(jnp.float32)[None, :]
        query_incoming = low(query_block * jnp.transpose(entry_weight)[:, :, None])
        exit_weight = exit_rate * (segment_block == last_segment).astype(jnp.float32)[None, :]
        key_projected = low(key_block * jnp.transpose(exit_weight)[:, :, None])
        layer_result = jnp.einsum('hnm,mhv->nhv', mixing, value_tile_rows, precision=MAXIMUM_ACCURACY)
        layer_result = layer_result + jnp.einsum('ced,edw->cew', query_incoming, low(retention_state), precision=MAXIMUM_ACCURACY)
        state_increment = low_back(jnp.einsum('tdr,tdq->drq', key_projected, value_tile_rows, precision=MAXIMUM_ACCURACY))
        carried = whole_rate * (last_segment == before).astype(jnp.float32)
        return ((carried[:, None, None] * retention_state + state_increment, last_segment), layer_result)
    initial = (jnp.zeros((head_count, key_size, value_size), jnp.float32), jnp.array(-1, jnp.int32))
    pieces = (queries.reshape(blocks, block_size, head_count, key_size), keys_in.reshape(blocks, block_size, head_count, key_size), values.reshape(blocks, block_size, head_count, value_size), segments.reshape(blocks, block_size))
    final_carry, results = lax.scan(block_step, initial, pieces)
    return results.reshape(length, head_count, value_size)

def block_forward(tokens, weights, cosine_table, sine_table, segments):
    prescale, query_weight, key_weight, value_weight, gate_weight, groupscale, groupshift, output_weight, postscale, postshift, expand_weight, hiddenbias, reduce_weight, outputbias = weights
    row_count = tokens.shape[0]
    inverse = lax.rsqrt(lax.optimization_barrier(jnp.mean(tokens * tokens, axis=-1, keepdims=True)) + 1e-06)
    normed = low(tokens * inverse * prescale)
    query_pre = low_back(jnp.dot(normed, query_weight, precision=MAXIMUM_ACCURACY))
    key_pre = low_back(jnp.dot(normed, key_weight, precision=MAXIMUM_ACCURACY))
    value_all = low(low_back(jnp.dot(normed, value_weight, precision=MAXIMUM_ACCURACY)))
    gate_pre = low_back(jnp.dot(normed, gate_weight, precision=MAXIMUM_ACCURACY))
    queries = low(rotate(query_pre.reshape(row_count, HEADS, KEY), cosine_table, sine_table))
    keys_in = low(rotate(key_pre.reshape(row_count, HEADS, KEY), cosine_table, sine_table) * KEY ** (-0.5))
    retained = low_back(retention(queries, keys_in, value_all.reshape(row_count, HEADS, VAL), segments, decay_logs(HEADS, 0), TOK_DEV))
    centred = retained - lax.optimization_barrier(jnp.mean(retained, axis=-1, keepdims=True))
    unit_norm = centred * lax.rsqrt(lax.optimization_barrier(jnp.mean(centred * centred, axis=-1, keepdims=True)) + 1.0)
    grouped = unit_norm.reshape(row_count, HV) * groupscale + groupshift
    gated_out = low(jax.nn.silu(gate_pre) * grouped)
    branch = low_back(jnp.dot(gated_out, output_weight, precision=MAXIMUM_ACCURACY))
    residual = tokens + branch
    shifted = residual - lax.optimization_barrier(jnp.mean(residual, axis=-1, keepdims=True))
    standard = shifted * lax.rsqrt(lax.optimization_barrier(jnp.mean(shifted * shifted, axis=-1, keepdims=True)) + 1e-05)
    layered = low(standard * postscale + postshift)
    hidden = low_back(jnp.dot(layered, expand_weight, precision=MAXIMUM_ACCURACY) + hiddenbias)
    active = low(jax.nn.gelu(hidden, approximate=False))
    return residual + jnp.dot(active, reduce_weight, precision=MAXIMUM_ACCURACY) + outputbias

def reference(tokens, prescale, query_weight, key_weight, value_weight, gate_weight, groupscale, groupshift, output_weight, postscale, postshift, expand_weight, hiddenbias, reduce_weight, outputbias, cotangent, doc_lengths, segments):
    params = tuple((element.astype(jnp.float32) for element in (prescale, query_weight, key_weight, value_weight, gate_weight, groupscale, groupshift, output_weight, postscale, postshift, expand_weight, hiddenbias, reduce_weight, outputbias)))
    doc_lengths = doc_lengths.astype(jnp.int32)
    segments = segments.astype(jnp.int32)

    def per_stream(summed_in, stream_data):
        stream_tokens, stream_cotangent, stream_lengths, stream_segments = stream_data
        positions = doc_positions(stream_lengths, 0, STREAM)
        cosine_table, sine_table = rotation_tables(positions, KEY)

        def forward(inputs, weights):
            return block_forward(inputs, weights, cosine_table[:, None, :], sine_table[:, None, :], stream_segments)
        output, pullback = jax.vjp(forward, stream_tokens.astype(jnp.float32), params)
        input_grad, weight_grads = pullback(stream_cotangent.astype(jnp.float32))
        summed_out = tuple((summed + gradient for summed, gradient in zip(summed_in, weight_grads)))
        return (summed_out, (output.astype(jnp.bfloat16), input_grad))
    initial = tuple((jnp.zeros_like(element) for element in params))
    totals, (outputs, input_grads) = lax.scan(per_stream, initial, (tokens, cotangent, doc_lengths, segments))
    return (outputs, input_grads, totals[0], totals[1], totals[2], totals[3], totals[4], totals[5], totals[6], totals[7], totals[8], totals[9], totals[10], totals[11], totals[12], totals[13])
```

```python
import math

import jax
import jax.numpy as jnp
from jax import lax
from jax.sharding import PartitionSpec as P

KEY = 256
VAL = 512
F32 = jnp.float32
BF16 = jnp.bfloat16


def swap_core(value):
    return lax.ppermute(value, "head", [(0, 1), (1, 0)])


def swap_batch(value, mask):
    return lax.ppermute(value, "batch", [(place, place ^ mask) for place in range(4)])


def spread(piece):
    middle = piece.shape[0] // 2
    first = swap_batch(piece, 1)
    second = swap_batch(piece, 2)
    upper = swap_batch(first[:middle], 2)
    lower = swap_batch(second[middle:], 1)
    return first, second, jnp.concatenate([upper, lower], axis=0)


def fold(parts):
    middle = parts[3].shape[0] // 2
    far = parts[3].astype(BF16)
    upper = swap_batch(far[:middle], 1)
    lower = swap_batch(far[middle:], 2)
    to_first = jnp.concatenate(
        [parts[1][:middle], parts[1][middle:] + lower.astype(F32)], axis=0
    ).astype(BF16)
    to_second = jnp.concatenate(
        [parts[2][:middle] + upper.astype(F32), parts[2][middle:]], axis=0
    ).astype(BF16)
    first = swap_batch(to_first, 1)
    second = swap_batch(to_second, 2)
    return parts[0] + first.astype(F32) + second.astype(F32)


def total(value):
    for axis in ("batch", "seq"):
        count = lax.axis_size(axis)
        step = 1
        while step < count:
            moved = lax.ppermute(value, axis, [(place, place ^ step) for place in range(count)])
            value = value + moved
            step *= 2
    return value


def hop(value, source, target):
    return lax.ppermute(value, "seq", [(source, target)])


def carry(keep, added, forward):
    count = lax.axis_size("seq")
    entered = []
    for chunk in range(0, 4, 2):
        factor = keep[chunk : chunk + 2, None, None]
        own = added[chunk : chunk + 2]
        state = jnp.zeros(own.shape, BF16)
        for step in range(count - 1):
            sent = (factor * state.astype(F32) + own).astype(BF16)
            source, target = (step, step + 1) if forward else (count - 1 - step, count - 2 - step)
            state = state + hop(sent, source, target)
        entered.append(state)
    return jnp.concatenate(entered, axis=0)


def dot(left, right):
    return jnp.dot(left, right, preferred_element_type=F32)


def contract_rows(left, right):
    return lax.dot_general(left, right, (((0,), (0,)), ((), ())), preferred_element_type=F32)


def contract_cols(left, right):
    return lax.dot_general(left, right, (((1,), (1,)), ((), ())), preferred_element_type=F32)


def normalize_back(grad_unit, unit_norm, inverse):
    mean_grad = jnp.mean(grad_unit, axis=-1, keepdims=True)
    mean_cross = jnp.mean(grad_unit * unit_norm, axis=-1, keepdims=True)
    return inverse * (grad_unit - mean_grad - unit_norm * mean_cross)


def rotate(values, cosine, sine, sign):
    middle = values.shape[-1] // 2
    former, latter = (values[..., :middle], values[..., middle:])
    return jnp.concatenate(
        [former * cosine - sign * latter * sine, latter * cosine + sign * former * sine], axis=-1
    )


def batched(subscripts, left, right):
    return jnp.einsum(subscripts, left, right, preferred_element_type=F32)


def place_columns(pieces, place, width):
    rows = pieces[0].shape[0]
    result = jnp.zeros((rows, 4 * width), F32)
    for slot, piece in enumerate(pieces):
        result = lax.dynamic_update_slice(result, piece.astype(F32), (0, (place ^ slot) * width))
    return result


def place_rows(pieces, place, height):
    result = jnp.zeros((4 * height, pieces[0].shape[1]), F32)
    for slot, piece in enumerate(pieces):
        result = lax.dynamic_update_slice(result, piece.astype(F32), ((place ^ slot) * height, 0))
    return result


def body(
    tokens,
    prescale,
    query_weight,
    key_weight,
    value_weight,
    gate_weight,
    groupscale,
    groupshift,
    output_weight,
    postscale,
    postshift,
    expand_weight,
    hiddenbias,
    reduce_weight,
    outputbias,
    cotangent,
    doc_lengths,
    segments,
):
    _, rows, width = tokens.shape
    half = rows // 2
    part = hiddenbias.shape[0] // 4
    core = lax.axis_index("head")
    place = lax.axis_index("batch")
    block = lax.axis_index("seq")

    def own_rows(value):
        return lax.dynamic_slice_in_dim(value, core * half, half, 0)

    def far_rows(value):
        return lax.dynamic_slice_in_dim(value, (1 - core) * half, half, 0)

    def cols_of(weight, size):
        return lax.dynamic_slice_in_dim(weight, place * size, size, 1)

    def rows_of(weight, size):
        return lax.dynamic_slice_in_dim(weight, place * size, size, 0)

    def gather_rows(weight):
        return lax.all_gather(weight, "seq", axis=0, tiled=True)

    def gather_cols(weight):
        return lax.all_gather(weight, "seq", axis=1, tiled=True)

    def scatter(grad, dimension):
        return lax.psum_scatter(grad.astype(BF16), "seq", scatter_dimension=dimension, tiled=True)

    key_value = gather_rows(
        jnp.concatenate([cols_of(key_weight, KEY), cols_of(value_weight, VAL)], axis=1)
    )
    query_gate = gather_rows(
        jnp.concatenate([cols_of(query_weight, KEY), cols_of(gate_weight, VAL)], axis=1)
    )
    output_own = gather_cols(rows_of(output_weight, VAL))
    expand_own = gather_rows(cols_of(expand_weight, part))
    reduce_own = gather_cols(rows_of(reduce_weight, part))

    tokens_own, tokens_far = own_rows(tokens[0]), far_rows(tokens[0])
    before = jnp.where(block == 0, -1, lax.ppermute(
        segments[0, rows - 1 :],
        "seq",
        [(source, source + 1) for source in range(lax.axis_size("seq") - 1)],
    ))
    marks = jnp.concatenate([segments[0], doc_lengths[0], before])[None]
    marks = jnp.concatenate([marks, swap_batch(marks, 1)], axis=0)
    marks = jnp.concatenate([marks, swap_batch(marks, 2)], axis=0)
    arrived = spread(tokens_own)
    pieces = [tokens_own, tokens_far]
    for piece in arrived:
        pieces += [piece, swap_core(piece)]
    dy = cotangent[0]
    dy_own = own_rows(dy)
    dy_rows = jnp.concatenate((dy_own,) + spread(dy_own), axis=0)

    inputs = jnp.concatenate(pieces, axis=0).astype(F32)
    inverse = lax.rsqrt(jnp.mean(inputs * inputs, axis=-1, keepdims=True) + 1e-06)
    normed = (inputs * inverse * prescale).astype(BF16)

    spans = marks[:, rows:-1]
    before = marks[:, -1]
    natural = marks[:, :rows]
    last = natural[:, rows - 1]
    segment = jnp.where(
        core == 0, natural, jnp.concatenate([natural[:, half:], natural[:, :half]], axis=1)
    )
    steps = jnp.arange(half, dtype=jnp.int32)
    index = jnp.concatenate([core * half + steps, (1 - core) * half + steps])
    stream_index = block * rows + index
    ends = jnp.cumsum(spans, axis=1)
    starts = jnp.sum(
        jnp.where(ends[:, None, :] <= stream_index[None, :, None], spans[:, None, :], 0), axis=2
    )
    positions = (stream_index[None, :] - starts).astype(F32)
    middle = KEY // 2
    frequency = jnp.exp(-math.log(10000.0) * jnp.arange(middle, dtype=F32) / (middle - 1))
    phases = positions[..., None] * frequency
    cosine, sine = jnp.cos(phases), jnp.sin(phases)
    head = (core * 4 + place).astype(F32)
    log_rate = jnp.log1p(-jnp.exp2(-5.0 - head))
    distance = index[:, None] - index[None, :]
    causal = distance >= 0
    decays = jnp.exp(jnp.where(causal, distance, 0).astype(F32) * log_rate)
    linked = (segment[:, :, None] == segment[:, None, :]) & causal[None]
    decay_matrix = jnp.where(linked, decays[None], 0.0)
    entry = jnp.exp((index + 1).astype(F32) * log_rate)[None] * (
        segment == before[:, None]
    ).astype(F32)
    exit_weight = jnp.exp((rows - 1 - index).astype(F32) * log_rate)[None] * (
        segment == last[:, None]
    ).astype(F32)
    entry, exit_weight = entry[..., None], exit_weight[..., None]
    keep = jnp.exp(rows * log_rate) * (last == before).astype(F32)

    key_value_pre = dot(normed, key_value)
    keys_in = (
        rotate(key_value_pre[:, :KEY].reshape(4, rows, KEY), cosine, sine, 1.0) * KEY ** (-0.5)
    ).astype(BF16)
    values = key_value_pre[:, KEY:].astype(BF16).reshape(4, rows, VAL)
    key_out = (keys_in.astype(F32) * exit_weight).astype(BF16)
    memory = carry(keep, batched("bmk,bmv->bkv", key_out, values), True)
    query_gate_pre = dot(normed, query_gate)
    queries = rotate(
        query_gate_pre[:, :KEY].reshape(4, rows, KEY), cosine, sine, 1.0
    ).astype(BF16)
    gate_pre = query_gate_pre[:, KEY:]
    query_in = (queries.astype(F32) * entry).astype(BF16)
    mixing = (batched("bnk,bmk->bnm", queries, keys_in) * decay_matrix).astype(BF16)
    retained = batched("bnm,bmv->bnv", mixing, values) + batched(
        "bnk,bkv->bnv", query_in, memory
    )
    retained = retained.reshape(4 * rows, VAL)
    centred = retained - jnp.mean(retained, axis=-1, keepdims=True)
    group_inverse = lax.rsqrt(jnp.mean(centred * centred, axis=-1, keepdims=True) + 1.0)
    unit_norm = centred * group_inverse
    scale_own = lax.dynamic_slice_in_dim(groupscale, place * VAL, VAL, 0)
    shift_own = lax.dynamic_slice_in_dim(groupshift, place * VAL, VAL, 0)
    grouped = unit_norm * scale_own + shift_own
    sigmoid = jax.nn.sigmoid(gate_pre)
    swish = gate_pre * sigmoid
    gated = (swish * grouped).astype(BF16).reshape(4, 2, half, VAL)
    gated_far = swap_core(gated[:, 1])
    gated_both = jnp.concatenate([gated[:, 0], gated_far], axis=-1).reshape(4 * half, 2 * VAL)

    output_both = jnp.concatenate([output_own, swap_core(output_own)], axis=0)
    expand_both = jnp.concatenate([expand_own, swap_core(expand_own)], axis=1)
    reduce_both = jnp.concatenate([reduce_own, swap_core(reduce_own)], axis=0)
    bias_own = lax.dynamic_slice_in_dim(hiddenbias, place * part, part, 0)
    bias_both = jnp.concatenate([bias_own, swap_core(bias_own)], axis=0)

    def slots(value):
        return value.reshape(4, half, value.shape[-1])

    branch = fold(slots(dot(gated_both, output_both)))
    residual = tokens_own.astype(F32) + branch
    shifted = residual - jnp.mean(residual, axis=-1, keepdims=True)
    layer_inverse = lax.rsqrt(jnp.mean(shifted * shifted, axis=-1, keepdims=True) + 1e-05)
    standard = shifted * layer_inverse
    layered_own = (standard * postscale + postshift).astype(BF16)
    layered = jnp.concatenate((layered_own,) + spread(layered_own), axis=0)

    hidden = dot(layered, expand_both) + bias_both
    cumulative = 0.5 * (1.0 + lax.erf(hidden * 0.5**0.5))
    active = (hidden * cumulative).astype(BF16)
    expanded = fold(slots(dot(active, reduce_both)))
    output_rows = (residual + expanded + outputbias).astype(BF16)
    output_far = swap_core(output_rows)
    layer_output = jnp.where(
        core == 0,
        jnp.concatenate([output_rows, output_far], axis=0),
        jnp.concatenate([output_far, output_rows], axis=0),
    )

    def core_sum(grad, dimension):
        size = grad.shape[dimension] // 2
        own = lax.slice_in_dim(grad, 0, size, axis=dimension)
        far = lax.slice_in_dim(grad, size, 2 * size, axis=dimension)
        return own + swap_core(far.astype(BF16)).astype(F32)

    dy_wide = dy_own.astype(F32)
    outputbias_grad = jnp.sum(dy_wide, axis=0)
    reduce_grad = scatter(core_sum(contract_rows(active, dy_rows), 0), 1)
    grad_active = contract_cols(dy_rows, reduce_both)
    slope = cumulative + hidden * jnp.exp(-0.5 * hidden * hidden) * (0.5 / math.pi) ** 0.5
    grad_hidden = (grad_active * slope).astype(BF16)
    hiddenbias_grad = jnp.sum(grad_hidden.astype(F32), axis=0)
    grad_layered = fold(slots(contract_cols(grad_hidden, expand_both)))
    expand_grad = scatter(core_sum(contract_rows(layered, grad_hidden), 1), 0)
    postscale_grad = jnp.sum(grad_layered * standard, axis=0)
    postshift_grad = jnp.sum(grad_layered, axis=0)
    grad_residual = dy_wide + normalize_back(grad_layered * postscale, standard, layer_inverse)
    grad_branch_own = grad_residual.astype(BF16)
    grad_branch = jnp.concatenate((grad_branch_own,) + spread(grad_branch_own), axis=0)

    grad_gated_both = contract_cols(grad_branch, output_both).astype(BF16).reshape(4, half, 2 * VAL)
    grad_gated_far = swap_core(grad_gated_both[..., VAL:])
    grad_gated = (
        jnp.stack([grad_gated_both[..., :VAL], grad_gated_far], axis=1)
        .reshape(4 * rows, VAL)
        .astype(F32)
    )
    output_grad = scatter(core_sum(contract_rows(gated_both, grad_branch), 0), 1)
    grad_gate = (grad_gated * grouped * sigmoid * (1.0 + gate_pre * (1.0 - sigmoid))).astype(BF16)
    grad_grouped = grad_gated * swish
    groupscale_grad = jnp.sum(grad_grouped * unit_norm, axis=0)
    groupshift_grad = jnp.sum(grad_grouped, axis=0)
    grad_retained = normalize_back(grad_grouped * scale_own, unit_norm, group_inverse)
    grad_retained = grad_retained.astype(BF16).reshape(4, rows, VAL)
    grad_memory = carry(keep, batched("bnk,bnv->bkv", query_in, grad_retained), False)
    grad_scores = (batched("bnv,bmv->bnm", grad_retained, values) * decay_matrix).astype(BF16)
    grad_queries = batched("bnm,bmk->bnk", grad_scores, keys_in) + entry * batched(
        "bnv,bkv->bnk", grad_retained, memory
    )
    grad_query = rotate(grad_queries, cosine, sine, -1.0).astype(BF16).reshape(4 * rows, KEY)
    grad_query_gate = jnp.concatenate([grad_query, grad_gate], axis=1)
    query_gate_grad = scatter(contract_rows(normed, grad_query_gate), 0)
    grad_keys = batched("bnm,bnk->bmk", grad_scores, queries) + exit_weight * batched(
        "bmv,bkv->bmk", values, grad_memory
    )
    grad_values = batched("bnm,bnv->bmv", mixing, grad_retained) + batched(
        "bmk,bkv->bmv", key_out, grad_memory
    )
    grad_key = (rotate(grad_keys, cosine, sine, -1.0) * KEY ** (-0.5)).astype(BF16)
    grad_key_value = jnp.concatenate([grad_key, grad_values.astype(BF16)], axis=-1).reshape(
        4 * rows, KEY + VAL
    )
    key_value_grad = scatter(contract_rows(normed, grad_key_value), 0)
    grad_normed = contract_cols(grad_key_value, key_value) + contract_cols(
        grad_query_gate, query_gate
    )
    grad_normed = grad_normed.reshape(4, 2, half, width)
    grad_normed = fold(
        grad_normed[:, 0] + swap_core(grad_normed[:, 1].astype(BF16)).astype(F32)
    )
    inverse_own = inverse[:half]
    scaled = tokens_own.astype(F32) * inverse_own
    prescale_grad = jnp.sum(grad_normed * scaled, axis=0)
    grad_scaled = grad_normed * prescale
    grad_rows = grad_residual + inverse_own * (
        grad_scaled - scaled * jnp.mean(grad_scaled * scaled, axis=-1, keepdims=True)
    )
    grad_far = swap_core(grad_rows)
    tokens_grad = jnp.where(
        core == 0,
        jnp.concatenate([grad_rows, grad_far], axis=0),
        jnp.concatenate([grad_far, grad_rows], axis=0),
    )

    over_cores = jnp.concatenate(
        [hiddenbias_grad[part:], postscale_grad, postshift_grad, outputbias_grad]
    )
    over_cores = swap_core(over_cores) + jnp.concatenate(
        [hiddenbias_grad[:part], postscale_grad, postshift_grad, outputbias_grad]
    )
    columns = [
        lax.dynamic_update_slice(jnp.zeros((4 * part,), F32), piece, (place * part,))
        for piece in (over_cores[:part], groupscale_grad, groupshift_grad)
    ]
    sums = total(jnp.concatenate([over_cores[part:]] + columns))
    cuts = [width, 2 * width, 3 * width, 3 * width + 4 * part, 3 * width + 8 * part]
    postscale_sum, postshift_sum, outputbias_sum, hiddenbias_sum, scale_sum, shift_sum = jnp.split(
        sums, cuts
    )
    prescale_sum = total(prescale_grad + swap_core(prescale_grad))

    def all_pieces(grad):
        return (grad,) + spread(grad)

    reduce_pieces = all_pieces(reduce_grad)
    expand_pieces = all_pieces(expand_grad)
    output_pieces = all_pieces(output_grad)
    query_gate_pieces = all_pieces(query_gate_grad)
    key_value_pieces = all_pieces(key_value_grad)
    return (
        layer_output[None],
        tokens_grad[None],
        prescale_sum,
        place_columns([piece[:, :KEY] for piece in query_gate_pieces], place, KEY),
        place_columns([piece[:, :KEY] for piece in key_value_pieces], place, KEY),
        place_columns([piece[:, KEY:] for piece in key_value_pieces], place, VAL),
        place_columns([piece[:, KEY:] for piece in query_gate_pieces], place, VAL),
        scale_sum,
        shift_sum,
        place_rows(output_pieces, place, VAL),
        postscale_sum,
        postshift_sum,
        place_columns(expand_pieces, place, part),
        hiddenbias_sum,
        place_rows(reduce_pieces, place, part),
        outputbias_sum,
    )


def solution(mesh):
    in_specs = (
        P("batch", "seq", None),
        P(),
        P("seq", "head"),
        P("seq", "head"),
        P("seq", "head"),
        P("seq", "head"),
        P("head"),
        P("head"),
        P("head", "seq"),
        P(),
        P(),
        P("seq", "head"),
        P("head"),
        P("head", "seq"),
        P(),
        P("batch", "seq", None),
        P("batch", None),
        P("batch", "seq"),
    )
    out_specs = (
        P("batch", "seq", None),
        P("batch", "seq", None),
        P(),
        P("seq", "head"),
        P("seq", "head"),
        P("seq", "head"),
        P("seq", "head"),
        P("head"),
        P("head"),
        P("head", "seq"),
        P(),
        P(),
        P("seq", "head"),
        P("head"),
        P("head", "seq"),
        P(),
    )
    return jax.shard_map(body, mesh=mesh, in_specs=in_specs, out_specs=out_specs, check_vma=False)
```

```python
import math

import jax
import jax.numpy as jnp
from jax import lax
from jax.experimental import pallas as pl
from jax.experimental.pallas import tpu as pltpu
from jax.sharding import PartitionSpec as P

KEY = 256
VAL = 512
F32 = jnp.float32
BF16 = jnp.bfloat16


def swap_core(value):
    return lax.ppermute(value, "head", [(0, 1), (1, 0)])


def swap_batch(value, mask):
    return lax.ppermute(value, "batch", [(place, place ^ mask) for place in range(4)])


def after(value, *earlier):
    return lax.optimization_barrier((value,) + earlier)[0]


def spread(piece):
    middle = piece.shape[0] // 2
    first = swap_batch(piece, 1)
    second = swap_batch(piece, 2)
    upper = swap_batch(first[:middle], 2)
    lower = swap_batch(second[middle:], 1)
    return first, second, jnp.concatenate([upper, lower], axis=0)


def fold(parts):
    middle = parts[3].shape[0] // 2
    far = parts[3]
    upper = swap_batch(far[:middle], 1)
    lower = swap_batch(far[middle:], 2)
    to_first = jnp.concatenate(
        [parts[1][:middle], parts[1][middle:] + lower.astype(F32)], axis=0
    ).astype(BF16)
    to_second = jnp.concatenate(
        [parts[2][:middle] + upper.astype(F32), parts[2][middle:]], axis=0
    ).astype(BF16)
    first = swap_batch(to_first, 1)
    second = swap_batch(to_second, 2)
    return parts[0] + first.astype(F32) + second.astype(F32)


def total(value):
    for axis in ("batch", "seq"):
        count = lax.axis_size(axis)
        step = 1
        while step < count:
            moved = lax.ppermute(value, axis, [(place, place ^ step) for place in range(count)])
            value = value + moved
            step *= 2
    return value


def turn(value, steps):
    count = lax.axis_size("seq")
    return lax.ppermute(
        value, "seq", [(source, (source + steps) % count) for source in range(count)]
    )


def hop(value, source, target):
    return lax.ppermute(value, "seq", [(source, target)])


def carry(keep, added, forward):
    count = lax.axis_size("seq")
    entered = []
    for chunk in range(0, 4, 2):
        factor = keep[chunk : chunk + 2, None, None]
        own = added[chunk : chunk + 2]
        state = jnp.zeros(own.shape, BF16)
        for step in range(count - 1):
            sent = (factor * state.astype(F32) + own).astype(BF16)
            source, target = (step, step + 1) if forward else (count - 1 - step, count - 2 - step)
            state = state + hop(sent, source, target)
        entered.append(state)
    return jnp.concatenate(entered, axis=0)


def dot(left, right):
    return jnp.dot(left, right, preferred_element_type=F32)


def contract_rows(left, right):
    return lax.dot_general(left, right, (((0,), (0,)), ((), ())), preferred_element_type=F32)


def contract_cols(left, right):
    return lax.dot_general(left, right, (((1,), (1,)), ((), ())), preferred_element_type=F32)


def normalize_back(grad_unit, unit_norm, inverse):
    mean_grad = jnp.mean(grad_unit, axis=-1, keepdims=True)
    mean_cross = jnp.mean(grad_unit * unit_norm, axis=-1, keepdims=True)
    return inverse * (grad_unit - mean_grad - unit_norm * mean_cross)


def rotated(values, cosine, sine):
    middle = values.shape[-1] // 2
    former, latter = (values[:, :middle], values[:, middle:])
    return jnp.concatenate(
        [former * cosine - latter * sine, latter * cosine + former * sine], axis=-1
    )


def flat(ref):
    value = ref[...]
    return value.reshape(-1, value.shape[-1])


def put(ref, value):
    ref[...] = value.reshape(ref.shape).astype(ref.dtype)


def weigh(value, weight):
    return (value.astype(F32) * weight).astype(BF16)


def decay_of(columns, lines, rate):
    distance = columns[:, 3:4] - lines[1:2]
    linked = (columns[:, 2:3] == lines[0:1]) & (distance >= 0)
    return jnp.where(linked, jnp.exp(jnp.maximum(distance, 0.0) * rate), 0.0)


def key_value_kernel(normed, weight, cosine, sine, columns, keys, values, added):
    product = dot(flat(normed), weight[...])
    key = (rotated(product[:, :KEY], flat(cosine), flat(sine)) * KEY ** (-0.5)).astype(BF16)
    value = product[:, KEY:].astype(BF16)
    put(keys, key)
    put(values, value)
    put(added, contract_rows(weigh(key, flat(columns)[:, 1:2]), value))


def retain_kernel(
    normed, weight, cosine, sine, columns, lines, rate, keys, values, memory, scale, shift,
    queries, gate, unit, inverse, gated,
):
    product = dot(flat(normed), weight[...])
    query = rotated(product[:, :KEY], flat(cosine), flat(sine)).astype(BF16)
    table = flat(columns)
    decay = decay_of(table, flat(lines), rate[...])
    mixing = (contract_cols(query, flat(keys)) * decay).astype(BF16)
    retained = dot(mixing, flat(values)) + dot(weigh(query, table[:, 0:1]), flat(memory))
    centred = retained - jnp.mean(retained, axis=-1, keepdims=True)
    factor = lax.rsqrt(jnp.mean(centred * centred, axis=-1, keepdims=True) + 1.0)
    unit_norm = centred * factor
    gate_pre = product[:, KEY:]
    put(queries, query)
    put(gate, gate_pre)
    put(unit, unit_norm)
    put(inverse, factor)
    grouped = unit_norm * scale[...] + shift[...]
    put(gated, gate_pre * jax.nn.sigmoid(gate_pre) * grouped)


def gate_back_kernel(
    grad_own, grad_far, gate, unit, inverse, scale, shift, columns, queries,
    grad_gate, grad_retained, reach, sums,
):
    grad_gated = jnp.concatenate([flat(grad_own), flat(grad_far)], axis=0).astype(F32)
    gate_pre, unit_norm = flat(gate), flat(unit)
    grouped = unit_norm * scale[...] + shift[...]
    sigmoid = jax.nn.sigmoid(gate_pre)
    put(grad_gate, grad_gated * grouped * sigmoid * (1.0 + gate_pre * (1.0 - sigmoid)))
    grad_grouped = grad_gated * (gate_pre * sigmoid)
    part = jnp.concatenate(
        [
            jnp.sum(grad_grouped * unit_norm, axis=0, keepdims=True),
            jnp.sum(grad_grouped, axis=0, keepdims=True),
        ],
        axis=0,
    )

    @pl.when(pl.program_id(0) == 0)
    def first():
        sums[...] = part

    @pl.when(pl.program_id(0) > 0)
    def later():
        sums[...] += part

    grad = normalize_back(grad_grouped * scale[...], unit_norm, flat(inverse)).astype(BF16)
    put(grad_retained, grad)
    put(reach, contract_rows(weigh(flat(queries), flat(columns)[:, 0:1]), grad))


def local_back_kernel(
    grad_retained, grad_gate, queries, keys, values, memory, columns, lines, rate, cosine, sine,
    grad_query_gate, grad_keys, grad_values,
):
    grad, query, key, value = flat(grad_retained), flat(queries), flat(keys), flat(values)
    table = flat(columns)
    decay = decay_of(table, flat(lines), rate[...])
    mixing = (contract_cols(query, key) * decay).astype(BF16)
    grad_scores = (contract_cols(grad, value) * decay).astype(BF16)
    grad_query = dot(grad_scores, key) + table[:, 0:1] * contract_cols(grad, flat(memory))
    grad_query = rotated(grad_query, flat(cosine), -flat(sine)).astype(BF16)
    put(grad_query_gate, jnp.concatenate([grad_query, flat(grad_gate)], axis=-1))
    put(grad_keys, contract_rows(grad_scores, query))
    put(grad_values, contract_rows(mixing, grad))


def state_back_kernel(
    grad_keys, grad_values, keys, values, grad_memory, columns, cosine, sine, grad_key_value
):
    weight = flat(columns)[:, 1:2]
    state = flat(grad_memory)
    grad_key = flat(grad_keys) + weight * contract_cols(flat(values), state)
    grad_key = rotated(grad_key, flat(cosine), -flat(sine)) * KEY ** (-0.5)
    grad_value = flat(grad_values) + dot(weigh(flat(keys), weight), state)
    put(
        grad_key_value,
        jnp.concatenate([grad_key.astype(BF16), grad_value.astype(BF16)], axis=-1),
    )


def stream_kernel(
    normed, weight, cosine, sine, columns, lines, rate, scale, shift,
    queries, keys, values, memory, gate, unit, inverse, gated, state,
):
    @pl.when(pl.program_id(0) == 0)
    def first():
        state[...] = jnp.zeros_like(state)

    product = dot(flat(normed), weight[...])
    table = flat(columns)
    query = rotated(product[:, :KEY], flat(cosine), flat(sine)).astype(BF16)
    key = rotated(product[:, KEY : 2 * KEY], flat(cosine), flat(sine)) * KEY ** (-0.5)
    key = key.astype(BF16)
    value = product[:, 2 * KEY : 2 * KEY + VAL].astype(BF16)
    gate_pre = product[:, 2 * KEY + VAL :]
    low = state[...].astype(BF16)
    decay = decay_of(table, flat(lines), rate[...])
    mixing = (contract_cols(query, key) * decay).astype(BF16)
    retained = dot(mixing, value) + dot(weigh(query, table[:, 0:1]), low)
    state[...] = table[0:1, 4:5] * state[...] + contract_rows(weigh(key, table[:, 1:2]), value)
    centred = retained - jnp.mean(retained, axis=-1, keepdims=True)
    factor = lax.rsqrt(jnp.mean(centred * centred, axis=-1, keepdims=True) + 1.0)
    unit_norm = centred * factor
    put(queries, query)
    put(keys, key)
    put(values, value)
    put(memory, low)
    put(gate, gate_pre)
    put(unit, unit_norm)
    put(inverse, factor)
    grouped = unit_norm * scale[...] + shift[...]
    put(gated, gate_pre * jax.nn.sigmoid(gate_pre) * grouped)


def stream_back_kernel(
    grad_own, grad_far, gate, unit, inverse, scale, shift, columns, lines, rate, cosine, sine,
    queries, keys, values, memory, grads, sums, state,
):
    grad_gated = jnp.concatenate([flat(grad_own), flat(grad_far)], axis=0).astype(F32)
    gate_pre, unit_norm, table = flat(gate), flat(unit), flat(columns)
    query, key, value = flat(queries), flat(keys), flat(values)
    entry, weight = table[:, 0:1], table[:, 1:2]
    grouped = unit_norm * scale[...] + shift[...]
    sigmoid = jax.nn.sigmoid(gate_pre)
    grad_gate = grad_gated * grouped * sigmoid * (1.0 + gate_pre * (1.0 - sigmoid))
    grad_grouped = grad_gated * (gate_pre * sigmoid)

    @pl.when(pl.program_id(0) == 0)
    def first():
        state[...] = jnp.zeros_like(state)
        sums[...] = jnp.zeros_like(sums)

    sums[0:1] += jnp.sum(grad_grouped * unit_norm, axis=0, keepdims=True)
    sums[1:2] += jnp.sum(grad_grouped, axis=0, keepdims=True)
    grad = normalize_back(grad_grouped * scale[...], unit_norm, flat(inverse)).astype(BF16)
    decay = decay_of(table, flat(lines), rate[...])
    mixing = (contract_cols(query, key) * decay).astype(BF16)
    grad_scores = (contract_cols(grad, value) * decay).astype(BF16)
    low = state[...].astype(BF16)
    grad_query = dot(grad_scores, key) + entry * contract_cols(grad, flat(memory))
    grad_key = contract_rows(grad_scores, query) + weight * contract_cols(value, low)
    grad_value = contract_rows(mixing, grad) + dot(weigh(key, weight), low)
    state[...] = table[0:1, 4:5] * state[...] + contract_rows(weigh(query, entry), grad)
    cosines, sines = flat(cosine), -flat(sine)
    put(
        grads,
        jnp.concatenate(
            [
                rotated(grad_query, cosines, sines).astype(BF16),
                (rotated(grad_key, cosines, sines) * KEY ** (-0.5)).astype(BF16),
                grad_value.astype(BF16),
                grad_gate.astype(BF16),
            ],
            axis=-1,
        ),
    )


def rows_spec(value, whole=False):
    if whole:
        return pl.BlockSpec(value.shape, lambda slot: (0,) * len(value.shape))
    if len(value.shape) == 4:
        two, _, half, width = value.shape
        return pl.BlockSpec((two, 1, half, width), lambda slot: (0, slot, 0, 0))
    return pl.BlockSpec((1,) + value.shape[1:], lambda slot: (slot, 0, 0))


def block_spec(value, whole=False, last=False):
    if whole:
        return pl.BlockSpec(value.shape, lambda step: (0,) * len(value.shape))
    rank = len(value.shape)
    shape = value.shape[: rank - 3] + (1,) + value.shape[rank - 2 :]
    return pl.BlockSpec(
        shape, lambda step: (0,) * (rank - 3) + (3 - step if last else step,) + (0, 0)
    )


def by_block(kernel, inputs, shared, out_shapes, last, summed=0):
    outs = [jax.ShapeDtypeStruct(shape, dtype) for shape, dtype in out_shapes]
    return pl.pallas_call(
        kernel,
        grid=(4,),
        in_specs=[block_spec(v, at in shared, last) for at, v in enumerate(inputs)],
        out_specs=[block_spec(v, at >= len(outs) - summed, last) for at, v in enumerate(outs)],
        out_shape=outs,
        scratch_shapes=[pltpu.VMEM((KEY, VAL), F32)],
        compiler_params=pltpu.CompilerParams(
            dimension_semantics=("arbitrary",), vmem_limit_bytes=56 * 2**20
        ),
    )(*inputs)


def by_slot(kernel, slotted, shared, order, out_shapes, summed=0):
    inputs = tuple(slotted) + tuple(shared)
    specs = [rows_spec(v) for v in slotted] + [rows_spec(v, True) for v in shared]
    outs = [jax.ShapeDtypeStruct(shape, dtype) for shape, dtype in out_shapes]
    out_specs = [rows_spec(v, at >= len(outs) - summed) for at, v in enumerate(outs)]
    return pl.pallas_call(
        kernel,
        grid=(4,),
        in_specs=[specs[at] for at in order],
        out_specs=out_specs,
        out_shape=outs,
        compiler_params=pltpu.CompilerParams(
            dimension_semantics=("arbitrary",), vmem_limit_bytes=56 * 2**20
        ),
    )(*[inputs[at] for at in order])


def slot_products(product, left, right):
    size = left.shape[0] // 4
    far = product(left[3 * size :], right).astype(BF16)
    left, right, far = lax.optimization_barrier((left, right, far))
    near = product(left[size : 3 * size], right)
    own = product(left[:size], right)
    return [own, near[:size], near[size:], far]


def place_columns(pieces, place, width):
    rows = pieces[0].shape[0]
    result = jnp.zeros((rows, 4 * width), F32)
    for slot, piece in enumerate(pieces):
        result = lax.dynamic_update_slice(result, piece.astype(F32), (0, (place ^ slot) * width))
    return result


def place_rows(pieces, place, height):
    result = jnp.zeros((4 * height, pieces[0].shape[1]), F32)
    for slot, piece in enumerate(pieces):
        result = lax.dynamic_update_slice(result, piece.astype(F32), ((place ^ slot) * height, 0))
    return result


def body(
    tokens,
    prescale,
    query_weight,
    key_weight,
    value_weight,
    gate_weight,
    groupscale,
    groupshift,
    output_weight,
    postscale,
    postshift,
    expand_weight,
    hiddenbias,
    reduce_weight,
    outputbias,
    cotangent,
    doc_lengths,
    segments,
):
    _, rows, width = tokens.shape
    half = rows // 2
    part = hiddenbias.shape[0] // 4
    core = lax.axis_index("head")
    place = lax.axis_index("batch")
    block = lax.axis_index("seq")
    within = lax.axis_size("seq") == 4
    size = half // 4

    def shares_of(*values):
        def share(of):
            cut = [lax.dynamic_slice_in_dim(v, (2 * of + core) * size, size, 0) for v in values]
            return jnp.concatenate(cut + [marks], axis=0)

        held = [share(place)]
        held += [swap_batch(share(place ^ slot), slot) for slot in (1, 2, 3)]
        return jnp.stack(held)

    def plane_of(held):
        result = jnp.zeros(held.shape, held.dtype)
        for steps in range(4):
            moved = lax.dynamic_index_in_dim(held, place ^ ((block + steps) % 4), 0, True)
            if steps:
                moved = turn(moved, steps)
            result = lax.dynamic_update_slice_in_dim(result, moved, (block - steps) % 4, 0)
        return result

    def give_back(value, dtype):
        if not within:
            return both_rows(value, swap_core(value)).astype(dtype)
        value = value.reshape(4, size, width)
        held = jnp.zeros((4, size, width), value.dtype)
        for steps in range(4):
            moved = lax.dynamic_index_in_dim(value, (block - steps) % 4, 0, True)
            if steps:
                moved = turn(moved, -steps)
            held = lax.dynamic_update_slice_in_dim(held, moved, (block + steps) % 4, 0)
        own = []
        for slot in range(4):
            moved = lax.dynamic_index_in_dim(held, place ^ slot, 0, False)
            own.append(swap_batch(moved, slot) if slot else moved)
        own = jnp.stack(own)
        far = swap_core(own)
        result = jnp.zeros((8, size, width), dtype)
        for slot in range(4):
            for side, shared in ((core, own), (1 - core, far)):
                result = lax.dynamic_update_slice_in_dim(
                    result, shared[slot : slot + 1].astype(dtype), 2 * (place ^ slot) + side, 0
                )
        return result.reshape(rows, width)

    def both_rows(own, far):
        result = jnp.zeros((rows, width), own.dtype)
        result = lax.dynamic_update_slice_in_dim(result, own, core * half, 0)
        return lax.dynamic_update_slice_in_dim(result, far, (1 - core) * half, 0)

    def cols_of(weight, size):
        return lax.dynamic_slice_in_dim(weight, place * size, size, 1)

    def rows_of(weight, size):
        return lax.dynamic_slice_in_dim(weight, place * size, size, 0)

    def gather_rows(weight):
        return lax.all_gather(weight, "seq", axis=0, tiled=True)

    def gather_cols(weight):
        return lax.all_gather(weight, "seq", axis=1, tiled=True)

    def scatter(grad, dimension):
        return lax.psum_scatter(grad.astype(BF16), "seq", scatter_dimension=dimension, tiled=True)

    project = jnp.concatenate(
        [
            cols_of(query_weight, KEY),
            cols_of(key_weight, KEY),
            cols_of(value_weight, VAL),
            cols_of(gate_weight, VAL),
        ],
        axis=1,
    )
    tokens = after(tokens, project)
    project = gather_rows(project)

    steps = jnp.arange(half, dtype=jnp.int32)
    if within:
        lengths = doc_lengths[0]
        marks = jnp.concatenate([segments[0], lengths // 64, lengths % 64]).astype(BF16)
        marks = jnp.pad(marks[None], ((0, 7), (0, width - marks.shape[0])))
        held = shares_of(cotangent[0], tokens[0])
        held_dy, held = held[:, :size], held[:, size:]
        held = plane_of(held)
        tokens_own = held[:, :size].reshape(half, width)
        marks = held[:, size].astype(jnp.int32)
        natural = marks[:, :rows]
        count = doc_lengths.shape[1]
        spans = marks[:, rows : rows + count] * 64 + marks[:, rows + count : rows + 2 * count]
        before = jnp.concatenate([jnp.full((1,), -1, jnp.int32), natural[:-1, rows - 1]])
        side, slot = jnp.arange(2)[:, None], jnp.arange(4)[None]
        share = 2 * (place ^ slot) + (core ^ side)
        index = share[:, :, None, None] * size + steps[:size]
        segment = jnp.take(natural.reshape(4, 8, size), share.reshape(8), axis=1)
        segment = segment.transpose(1, 0, 2).reshape(2, 4, 4, size)
        index = jnp.broadcast_to(index, segment.shape)
        at_block = jnp.arange(4)[None, None, :, None]
        stream_index = at_block * rows + index
        form = (1, 1, 4, 1)
    else:
        before = lax.ppermute(
            segments[0, rows - 1 :],
            "seq",
            [(source, source + 1) for source in range(lax.axis_size("seq") - 1)],
        )
        before = jnp.where(block == 0, -1, before)
        marks = jnp.concatenate([segments[0], doc_lengths[0], before])[None]
        marks = jnp.concatenate([marks, swap_batch(marks, 1)], axis=0)
        marks = jnp.concatenate([marks, swap_batch(marks, 2)], axis=0)
        natural, spans, before = marks[:, :rows], marks[:, rows:-1], marks[:, -1]
        tokens_own = lax.dynamic_slice_in_dim(tokens[0], core * half, half, 0)
        dy_own = lax.dynamic_slice_in_dim(cotangent[0], core * half, half, 0)
        index = jnp.stack([core * half + steps, (1 - core) * half + steps])[:, None]
        upper, lower = natural[None, :, :half], natural[None, :, half:]
        segment = jnp.where(
            core == 0,
            jnp.concatenate([upper, lower], axis=0),
            jnp.concatenate([lower, upper], axis=0),
        )
        index = jnp.broadcast_to(index, segment.shape)
        stream_index = block * rows + index
        form = (1, 4, 1)
    wide = tokens_own.astype(F32)
    inverse = lax.rsqrt(jnp.mean(wide * wide, axis=-1, keepdims=True) + 1e-06)
    scaled = wide * inverse
    normed_own = lax.optimization_barrier((scaled * prescale).astype(BF16))
    arrived = spread(normed_own)
    if within:
        dy_own = plane_of(after(held_dy, arrived[0])).reshape(half, width)
    normed = (normed_own,) + arrived
    normed = jnp.concatenate(normed + tuple(swap_core(piece) for piece in normed), axis=0)
    normed = lax.optimization_barrier(normed)
    dy_rows = jnp.concatenate((dy_own,) + spread(after(dy_own, arrived)), axis=0)
    output_own = gather_cols(after(rows_of(output_weight, VAL), arrived))
    expand_own = gather_rows(after(cols_of(expand_weight, part), dy_own))
    reduce_own = gather_cols(after(rows_of(reduce_weight, part), dy_rows))

    last = natural[:, rows - 1]
    ends = jnp.cumsum(spans, axis=1).reshape(form + (-1,))
    spans = spans.reshape(form + (-1,))
    starts = jnp.sum(jnp.where(ends <= stream_index[..., None], spans, 0), axis=-1)
    positions = (stream_index - starts).astype(F32)
    middle = KEY // 2
    frequency = jnp.exp(-math.log(10000.0) * jnp.arange(middle, dtype=F32) / (middle - 1))
    phases = positions[..., None] * frequency
    cosine, sine = jnp.cos(phases), jnp.sin(phases)
    head = (core * 4 + place).astype(F32)
    log_rate = jnp.log1p(-jnp.exp2(-5.0 - head))
    entry = jnp.exp((index + 1).astype(F32) * log_rate) * (
        segment == before.reshape(form)
    ).astype(F32)
    exit_weight = jnp.exp((rows - 1 - index).astype(F32) * log_rate) * (
        segment == last.reshape(form)
    ).astype(F32)
    keep = jnp.exp(rows * log_rate) * (last == before).astype(F32)
    segment, index = segment.astype(F32), index.astype(F32)
    wide_keep = jnp.broadcast_to(keep.reshape(form), segment.shape)
    columns = jnp.stack([entry, exit_weight, segment, index, wide_keep], axis=-1)
    lines = jnp.stack([segment, index], axis=0)
    if within:
        lines = lines.transpose(3, 0, 1, 2, 4)
    else:
        lines = lines.transpose(2, 0, 1, 3)
    lines = lines.reshape(4, 2, rows)
    rate = jnp.full((1, 1), log_rate)
    cosine, sine, columns, lines = lax.optimization_barrier((cosine, sine, columns, lines))

    def rows_of_width(size, dtype=BF16):
        return (segment.shape + (size,), dtype)

    def entries(size, dtype=BF16):
        return ((4, KEY, size), dtype)

    scale_own = lax.dynamic_slice_in_dim(groupscale, place * VAL, VAL, 0)[None]
    shift_own = lax.dynamic_slice_in_dim(groupshift, place * VAL, VAL, 0)[None]
    normed_slots = normed.reshape(segment.shape + (width,))
    if within:
        queries, keys, values, memory, gate, unit, group_inverse, gated = by_block(
            stream_kernel,
            (normed_slots, project, cosine, sine, columns, lines, rate, scale_own, shift_own),
            (1, 6, 7, 8),
            (
                rows_of_width(KEY),
                rows_of_width(KEY),
                rows_of_width(VAL),
                entries(VAL),
                rows_of_width(VAL, F32),
                rows_of_width(VAL, F32),
                rows_of_width(1, F32),
                rows_of_width(VAL),
            ),
            False,
        )
    else:
        key_value = project[:, KEY : 2 * KEY + VAL]
        query_gate = jnp.concatenate([project[:, :KEY], project[:, 2 * KEY + VAL :]], axis=1)
        keys, values, added = by_slot(
            key_value_kernel,
            (normed_slots, cosine, sine, columns),
            (key_value,),
            (0, 4, 1, 2, 3),
            (rows_of_width(KEY), rows_of_width(VAL), entries(VAL, F32)),
        )
        memory = carry(keep, added, True)
        queries, gate, unit, group_inverse, gated = by_slot(
            retain_kernel,
            (normed_slots, cosine, sine, columns, lines, keys, values, memory),
            (query_gate, rate, scale_own, shift_own),
            (0, 8, 1, 2, 3, 4, 9, 5, 6, 7, 10, 11),
            (
                rows_of_width(KEY),
                rows_of_width(VAL, F32),
                rows_of_width(VAL, F32),
                rows_of_width(1, F32),
                rows_of_width(VAL),
            ),
        )
    gated_own = gated[0].reshape(4 * half, VAL)
    gated_far = swap_core(gated[1].reshape(4 * half, VAL))
    gated_both = jnp.concatenate([gated_own, gated_far], axis=-1)

    output_own = after(output_own, gated_both)
    output_both = jnp.concatenate([output_own, swap_core(output_own)], axis=0)
    bias_own = lax.dynamic_slice_in_dim(hiddenbias, place * part, part, 0)
    bias_both = jnp.concatenate([bias_own, swap_core(bias_own)], axis=0)

    branch = fold(slot_products(dot, gated_both, output_both))
    residual = wide + branch
    shifted = residual - jnp.mean(residual, axis=-1, keepdims=True)
    layer_inverse = lax.rsqrt(jnp.mean(shifted * shifted, axis=-1, keepdims=True) + 1e-05)
    standard = shifted * layer_inverse
    layered_own = (standard * postscale + postshift).astype(BF16)
    layered = jnp.concatenate((layered_own,) + spread(layered_own), axis=0)
    expand_own = after(expand_own, layered_own)
    expand_both = jnp.concatenate([expand_own, swap_core(expand_own)], axis=1)
    reduce_own = after(reduce_own, expand_own)
    reduce_both = jnp.concatenate([reduce_own, swap_core(reduce_own)], axis=0)

    hidden = dot(layered, expand_both) + bias_both
    cumulative = 0.5 * (1.0 + lax.erf(hidden * 0.5**0.5))
    active = (hidden * cumulative).astype(BF16)
    def core_sum(grad, dimension):
        size = grad.shape[dimension] // 2
        own = lax.slice_in_dim(grad, 0, size, axis=dimension)
        far = lax.slice_in_dim(grad, size, 2 * size, axis=dimension)
        return own + swap_core(far.astype(BF16)).astype(F32)

    dy_wide = dy_own.astype(F32)
    outputbias_grad = jnp.sum(dy_wide, axis=0)
    reduce_grad = scatter(core_sum(contract_rows(active, dy_rows), 0), 1)
    grad_active = contract_cols(dy_rows, reduce_both)
    slope = cumulative + hidden * jnp.exp(-0.5 * hidden * hidden) * (0.5 / math.pi) ** 0.5
    grad_hidden = (grad_active * slope).astype(BF16)
    hiddenbias_grad = jnp.sum(grad_hidden.astype(F32), axis=0)
    grad_layered = fold(slot_products(contract_cols, grad_hidden, expand_both))
    expand_grad = scatter(core_sum(contract_rows(layered, grad_hidden), 1), 0)
    postscale_grad = jnp.sum(grad_layered * standard, axis=0)
    postshift_grad = jnp.sum(grad_layered, axis=0)
    grad_residual = dy_wide + normalize_back(grad_layered * postscale, standard, layer_inverse)
    grad_branch_own = grad_residual.astype(BF16)
    grad_branch = jnp.concatenate((grad_branch_own,) + spread(grad_branch_own), axis=0)

    expanded = fold(slot_products(dot, after(active, grad_branch), reduce_both))
    output_rows = (residual + expanded + outputbias).astype(BF16)
    layer_output = give_back(output_rows, BF16)

    grad_gated_both = contract_cols(grad_branch, output_both).astype(BF16)
    grad_gated_own = grad_gated_both[:, :VAL].reshape(segment.shape[1:] + (VAL,))
    grad_gated_far = swap_core(grad_gated_both[:, VAL:]).reshape(segment.shape[1:] + (VAL,))
    output_grad = core_sum(contract_rows(gated_both, grad_branch), 0)
    if within:
        grads, group_sums = by_block(
            stream_back_kernel,
            (grad_gated_own, grad_gated_far, gate, unit, group_inverse, scale_own, shift_own)
            + (columns, lines, rate, cosine, sine, queries, keys, values, memory),
            (5, 6, 9),
            (rows_of_width(2 * KEY + 2 * VAL), ((2, VAL), F32)),
            True,
            summed=1,
        )
    else:
        grad_gate, grad_retained, reach, group_sums = by_slot(
            gate_back_kernel,
            (grad_gated_own, grad_gated_far, gate, unit, group_inverse, columns, queries),
            (scale_own, shift_own),
            (0, 1, 2, 3, 4, 7, 8, 5, 6),
            (rows_of_width(VAL), rows_of_width(VAL), entries(VAL, F32), ((2, VAL), F32)),
            summed=1,
        )
        grad_memory = carry(keep, reach, False)
        grad_query_gate, grad_keys, grad_values = by_slot(
            local_back_kernel,
            (grad_retained, grad_gate, queries, keys, values, memory, columns, lines)
            + (cosine, sine),
            (rate,),
            (0, 1, 2, 3, 4, 5, 6, 7, 10, 8, 9),
            (rows_of_width(KEY + VAL), rows_of_width(KEY, F32), rows_of_width(VAL, F32)),
        )
        (grad_key_value,) = by_slot(
            state_back_kernel,
            (grad_keys, grad_values, keys, values, grad_memory, columns, cosine, sine),
            (),
            range(8),
            (rows_of_width(KEY + VAL),),
        )
        grads = jnp.concatenate(
            [grad_query_gate[..., :KEY], grad_key_value, grad_query_gate[..., KEY:]], axis=-1
        )
    groupscale_grad, groupshift_grad = group_sums[0], group_sums[1]
    grads = grads.reshape(4 * rows, 2 * KEY + 2 * VAL)
    gate_grad = contract_rows(normed, grads[:, 2 * KEY + VAL :]).astype(BF16)
    first_grad = contract_rows(normed, grads[:, : 2 * KEY + VAL]).astype(BF16)
    grads = after(grads, gate_grad, first_grad)
    far_terms = contract_cols(grads[4 * half :], project).astype(BF16)
    far_terms = swap_core(far_terms).astype(F32)
    far_corner = contract_cols(grads[3 * half : 4 * half], project) + far_terms[3 * half :]
    own_terms = contract_cols(grads[: 3 * half], project) + far_terms[: 3 * half]
    own_terms = [own_terms[slot * half : (slot + 1) * half] for slot in range(3)]
    grad_normed = fold(own_terms + [far_corner.astype(BF16)])
    output_grad = scatter(output_grad, 1)
    gate_grad = scatter(gate_grad, 0)
    first_grad = scatter(first_grad, 0)
    prescale_grad = jnp.sum(grad_normed * scaled, axis=0)
    grad_scaled = grad_normed * prescale
    grad_rows = grad_residual + inverse * (
        grad_scaled - scaled * jnp.mean(grad_scaled * scaled, axis=-1, keepdims=True)
    )
    tokens_grad = give_back(grad_rows.astype(BF16) if within else grad_rows, F32)

    by_width = [prescale_grad, postscale_grad, postshift_grad, outputbias_grad]
    over_cores = swap_core(jnp.concatenate([hiddenbias_grad[part:]] + by_width))
    over_cores = over_cores + jnp.concatenate([hiddenbias_grad[:part]] + by_width)
    spaced = [
        lax.dynamic_update_slice(jnp.zeros((4 * part,), F32), piece, (place * part,))
        for piece in (over_cores[:part], groupscale_grad, groupshift_grad)
    ]
    sums = total(jnp.concatenate([over_cores[part:]] + spaced))
    cuts = [width * at for at in range(1, 5)] + [4 * width + 4 * part, 4 * width + 8 * part]
    prescale_sum, postscale_sum, postshift_sum, outputbias_sum, hiddenbias_sum, scale_sum, shift_sum = (
        jnp.split(sums, cuts)
    )

    def all_pieces(grad):
        return (grad,) + spread(grad)

    reduce_pieces = all_pieces(reduce_grad)
    expand_pieces = all_pieces(expand_grad)
    output_pieces = all_pieces(output_grad)
    gate_pieces = all_pieces(gate_grad)
    first_pieces = all_pieces(first_grad)
    return (
        layer_output[None],
        tokens_grad[None],
        prescale_sum,
        place_columns([piece[:, :KEY] for piece in first_pieces], place, KEY),
        place_columns([piece[:, KEY : 2 * KEY] for piece in first_pieces], place, KEY),
        place_columns([piece[:, 2 * KEY :] for piece in first_pieces], place, VAL),
        place_columns(gate_pieces, place, VAL),
        scale_sum,
        shift_sum,
        place_rows(output_pieces, place, VAL),
        postscale_sum,
        postshift_sum,
        place_columns(expand_pieces, place, part),
        hiddenbias_sum,
        place_rows(reduce_pieces, place, part),
        outputbias_sum,
    )


def solution(mesh):
    in_specs = (
        P("batch", "seq", None),
        P(),
        P("seq", "head"),
        P("seq", "head"),
        P("seq", "head"),
        P("seq", "head"),
        P("head"),
        P("head"),
        P("head", "seq"),
        P(),
        P(),
        P("seq", "head"),
        P("head"),
        P("head", "seq"),
        P(),
        P("batch", "seq", None),
        P("batch", None),
        P("batch", "seq"),
    )
    out_specs = (
        P("batch", "seq", None),
        P("batch", "seq", None),
        P(),
        P("seq", "head"),
        P("seq", "head"),
        P("seq", "head"),
        P("seq", "head"),
        P("head"),
        P("head"),
        P("head", "seq"),
        P(),
        P(),
        P("seq", "head"),
        P("head"),
        P("head", "seq"),
        P(),
    )
    return jax.shard_map(body, mesh=mesh, in_specs=in_specs, out_specs=out_specs, check_vma=False)
```

```python
import math

import jax
import jax.numpy as jnp
from jax import lax
from jax.experimental import pallas as pl
from jax.experimental.pallas import tpu as pltpu
from jax.sharding import PartitionSpec as P

KEY = 256
VAL = 512
F32 = jnp.float32
BF16 = jnp.bfloat16


def swap_core(value):
    return lax.ppermute(value, "head", [(0, 1), (1, 0)])


def swap_batch(value, mask):
    return lax.ppermute(value, "batch", [(place, place ^ mask) for place in range(4)])


def after(value, *earlier):
    return lax.optimization_barrier((value,) + earlier)[0]


def spread(piece):
    middle = piece.shape[0] // 2
    first = swap_batch(piece, 1)
    second = swap_batch(piece, 2)
    upper = swap_batch(first[:middle], 2)
    lower = swap_batch(second[middle:], 1)
    return first, second, jnp.concatenate([upper, lower], axis=0)


def fold(parts):
    middle = parts[3].shape[0] // 2
    far = parts[3]
    upper = swap_batch(far[:middle], 1)
    lower = swap_batch(far[middle:], 2)
    to_first = jnp.concatenate(
        [parts[1][:middle], parts[1][middle:] + lower.astype(F32)], axis=0
    ).astype(BF16)
    to_second = jnp.concatenate(
        [parts[2][:middle] + upper.astype(F32), parts[2][middle:]], axis=0
    ).astype(BF16)
    first = swap_batch(to_first, 1)
    second = swap_batch(to_second, 2)
    return parts[0] + first.astype(F32) + second.astype(F32)


def total(value):
    for axis in ("batch", "seq"):
        count = lax.axis_size(axis)
        step = 1
        while step < count:
            moved = lax.ppermute(value, axis, [(place, place ^ step) for place in range(count)])
            value = value + moved
            step *= 2
    return value


def turn(value, steps):
    count = lax.axis_size("seq")
    return lax.ppermute(
        value, "seq", [(source, (source + steps) % count) for source in range(count)]
    )


def hop(value, source, target):
    return lax.ppermute(value, "seq", [(source, target)])


def carry(keep, added, forward):
    count = lax.axis_size("seq")
    entered = []
    for chunk in range(0, 4, 2):
        factor = keep[chunk : chunk + 2, None, None]
        own = added[chunk : chunk + 2]
        state = jnp.zeros(own.shape, BF16)
        for step in range(count - 1):
            sent = (factor * state.astype(F32) + own).astype(BF16)
            source, target = (step, step + 1) if forward else (count - 1 - step, count - 2 - step)
            state = state + hop(sent, source, target)
        entered.append(state)
    return jnp.concatenate(entered, axis=0)


def dot(left, right):
    return jnp.dot(left, right, preferred_element_type=F32)


def contract_rows(left, right):
    return lax.dot_general(left, right, (((0,), (0,)), ((), ())), preferred_element_type=F32)


def contract_cols(left, right):
    return lax.dot_general(left, right, (((1,), (1,)), ((), ())), preferred_element_type=F32)


def normalize_back(grad_unit, unit_norm, inverse):
    mean_grad = jnp.mean(grad_unit, axis=-1, keepdims=True)
    mean_cross = jnp.mean(grad_unit * unit_norm, axis=-1, keepdims=True)
    return inverse * (grad_unit - mean_grad - unit_norm * mean_cross)


def rotated(values, cosine, sine):
    middle = values.shape[-1] // 2
    former, latter = (values[:, :middle], values[:, middle:])
    return jnp.concatenate(
        [former * cosine - latter * sine, latter * cosine + former * sine], axis=-1
    )


def flat(ref):
    value = ref[...]
    return value.reshape(-1, value.shape[-1])


def put(ref, value):
    ref[...] = value.reshape(ref.shape).astype(ref.dtype)


def weigh(value, weight):
    return (value.astype(F32) * weight).astype(BF16)


def decay_of(columns, lines, rate):
    distance = columns[:, 3:4] - lines[1:2]
    linked = (columns[:, 2:3] == lines[0:1]) & (distance >= 0)
    return jnp.where(linked, jnp.exp(jnp.maximum(distance, 0.0) * rate), 0.0)


def key_value_kernel(normed, weight, cosine, sine, columns, keys, values, added):
    product = dot(flat(normed), weight[...])
    key = (rotated(product[:, :KEY], flat(cosine), flat(sine)) * KEY ** (-0.5)).astype(BF16)
    value = product[:, KEY:].astype(BF16)
    put(keys, key)
    put(values, value)
    put(added, contract_rows(weigh(key, flat(columns)[:, 1:2]), value))


def retain_kernel(
    normed, weight, cosine, sine, columns, lines, rate, keys, values, memory, scale, shift,
    queries, gate, unit, inverse, gated,
):
    product = dot(flat(normed), weight[...])
    query = rotated(product[:, :KEY], flat(cosine), flat(sine)).astype(BF16)
    table = flat(columns)
    decay = decay_of(table, flat(lines), rate[...])
    mixing = (contract_cols(query, flat(keys)) * decay).astype(BF16)
    retained = dot(mixing, flat(values)) + dot(weigh(query, table[:, 0:1]), flat(memory))
    centred = retained - jnp.mean(retained, axis=-1, keepdims=True)
    factor = lax.rsqrt(jnp.mean(centred * centred, axis=-1, keepdims=True) + 1.0)
    unit_norm = centred * factor
    gate_pre = product[:, KEY:]
    put(queries, query)
    put(gate, gate_pre)
    put(unit, unit_norm)
    put(inverse, factor)
    grouped = unit_norm * scale[...] + shift[...]
    put(gated, gate_pre * jax.nn.sigmoid(gate_pre) * grouped)


def gate_back_kernel(
    grad_own, grad_far, gate, unit, inverse, scale, shift, columns, queries,
    grad_gate, grad_retained, reach, sums,
):
    grad_gated = jnp.concatenate([flat(grad_own), flat(grad_far)], axis=0).astype(F32)
    gate_pre, unit_norm = flat(gate), flat(unit)
    grouped = unit_norm * scale[...] + shift[...]
    sigmoid = jax.nn.sigmoid(gate_pre)
    put(grad_gate, grad_gated * grouped * sigmoid * (1.0 + gate_pre * (1.0 - sigmoid)))
    grad_grouped = grad_gated * (gate_pre * sigmoid)
    part = jnp.concatenate(
        [
            jnp.sum(grad_grouped * unit_norm, axis=0, keepdims=True),
            jnp.sum(grad_grouped, axis=0, keepdims=True),
        ],
        axis=0,
    )

    @pl.when(pl.program_id(0) == 0)
    def first():
        sums[...] = part

    @pl.when(pl.program_id(0) > 0)
    def later():
        sums[...] += part

    grad = normalize_back(grad_grouped * scale[...], unit_norm, flat(inverse)).astype(BF16)
    put(grad_retained, grad)
    put(reach, contract_rows(weigh(flat(queries), flat(columns)[:, 0:1]), grad))


def local_back_kernel(
    grad_retained, grad_gate, queries, keys, values, memory, columns, lines, rate, cosine, sine,
    grad_query_gate, grad_keys, grad_values,
):
    grad, query, key, value = flat(grad_retained), flat(queries), flat(keys), flat(values)
    table = flat(columns)
    decay = decay_of(table, flat(lines), rate[...])
    mixing = (contract_cols(query, key) * decay).astype(BF16)
    grad_scores = (contract_cols(grad, value) * decay).astype(BF16)
    grad_query = dot(grad_scores, key) + table[:, 0:1] * contract_cols(grad, flat(memory))
    grad_query = rotated(grad_query, flat(cosine), -flat(sine)).astype(BF16)
    put(grad_query_gate, jnp.concatenate([grad_query, flat(grad_gate)], axis=-1))
    put(grad_keys, contract_rows(grad_scores, query))
    put(grad_values, contract_rows(mixing, grad))


def state_back_kernel(
    grad_keys, grad_values, keys, values, grad_memory, columns, cosine, sine, grad_key_value
):
    weight = flat(columns)[:, 1:2]
    state = flat(grad_memory)
    grad_key = flat(grad_keys) + weight * contract_cols(flat(values), state)
    grad_key = rotated(grad_key, flat(cosine), -flat(sine)) * KEY ** (-0.5)
    grad_value = flat(grad_values) + dot(weigh(flat(keys), weight), state)
    put(
        grad_key_value,
        jnp.concatenate([grad_key.astype(BF16), grad_value.astype(BF16)], axis=-1),
    )


def stream_kernel(
    normed, weight, cosine, sine, columns, lines, rate, scale, shift,
    queries, keys, values, memory, gate, unit, inverse, gated, state,
):
    @pl.when(pl.program_id(0) == 0)
    def first():
        state[...] = jnp.zeros_like(state)

    product = dot(flat(normed), weight[...])
    table = flat(columns)
    query = rotated(product[:, :KEY], flat(cosine), flat(sine)).astype(BF16)
    key = rotated(product[:, KEY : 2 * KEY], flat(cosine), flat(sine)) * KEY ** (-0.5)
    key = key.astype(BF16)
    value = product[:, 2 * KEY : 2 * KEY + VAL].astype(BF16)
    gate_pre = product[:, 2 * KEY + VAL :]
    low = state[...].astype(BF16)
    decay = decay_of(table, flat(lines), rate[...])
    mixing = (contract_cols(query, key) * decay).astype(BF16)
    retained = dot(mixing, value) + dot(weigh(query, table[:, 0:1]), low)
    state[...] = table[0:1, 4:5] * state[...] + contract_rows(weigh(key, table[:, 1:2]), value)
    centred = retained - jnp.mean(retained, axis=-1, keepdims=True)
    factor = lax.rsqrt(jnp.mean(centred * centred, axis=-1, keepdims=True) + 1.0)
    unit_norm = centred * factor
    put(queries, query)
    put(keys, key)
    put(values, value)
    put(memory, low)
    put(gate, gate_pre)
    put(unit, unit_norm)
    put(inverse, factor)
    grouped = unit_norm * scale[...] + shift[...]
    put(gated, gate_pre * jax.nn.sigmoid(gate_pre) * grouped)


def stream_back_kernel(
    grad_own, grad_far, gate, unit, inverse, scale, shift, columns, lines, rate, cosine, sine,
    queries, keys, values, memory, grads, sums, state,
):
    grad_gated = jnp.concatenate([flat(grad_own), flat(grad_far)], axis=0).astype(F32)
    gate_pre, unit_norm, table = flat(gate), flat(unit), flat(columns)
    query, key, value = flat(queries), flat(keys), flat(values)
    entry, weight = table[:, 0:1], table[:, 1:2]
    grouped = unit_norm * scale[...] + shift[...]
    sigmoid = jax.nn.sigmoid(gate_pre)
    grad_gate = grad_gated * grouped * sigmoid * (1.0 + gate_pre * (1.0 - sigmoid))
    grad_grouped = grad_gated * (gate_pre * sigmoid)

    @pl.when(pl.program_id(0) == 0)
    def first():
        state[...] = jnp.zeros_like(state)
        sums[...] = jnp.zeros_like(sums)

    sums[0:1] += jnp.sum(grad_grouped * unit_norm, axis=0, keepdims=True)
    sums[1:2] += jnp.sum(grad_grouped, axis=0, keepdims=True)
    grad = normalize_back(grad_grouped * scale[...], unit_norm, flat(inverse)).astype(BF16)
    decay = decay_of(table, flat(lines), rate[...])
    mixing = (contract_cols(query, key) * decay).astype(BF16)
    grad_scores = (contract_cols(grad, value) * decay).astype(BF16)
    low = state[...].astype(BF16)
    grad_query = dot(grad_scores, key) + entry * contract_cols(grad, flat(memory))
    grad_key = contract_rows(grad_scores, query) + weight * contract_cols(value, low)
    grad_value = contract_rows(mixing, grad) + dot(weigh(key, weight), low)
    state[...] = table[0:1, 4:5] * state[...] + contract_rows(weigh(query, entry), grad)
    cosines, sines = flat(cosine), -flat(sine)
    put(
        grads,
        jnp.concatenate(
            [
                rotated(grad_query, cosines, sines).astype(BF16),
                (rotated(grad_key, cosines, sines) * KEY ** (-0.5)).astype(BF16),
                grad_value.astype(BF16),
                grad_gate.astype(BF16),
            ],
            axis=-1,
        ),
    )


def rows_spec(value, whole=False):
    if whole:
        return pl.BlockSpec(value.shape, lambda slot: (0,) * len(value.shape))
    if len(value.shape) == 4:
        two, _, half, width = value.shape
        return pl.BlockSpec((two, 1, half, width), lambda slot: (0, slot, 0, 0))
    return pl.BlockSpec((1,) + value.shape[1:], lambda slot: (slot, 0, 0))


def block_spec(value, whole=False, last=False):
    if whole:
        return pl.BlockSpec(value.shape, lambda step: (0,) * len(value.shape))
    rank = len(value.shape)
    shape = value.shape[: rank - 3] + (1,) + value.shape[rank - 2 :]
    return pl.BlockSpec(
        shape, lambda step: (0,) * (rank - 3) + (3 - step if last else step,) + (0, 0)
    )


def by_block(kernel, inputs, shared, out_shapes, last, summed=0):
    outs = [jax.ShapeDtypeStruct(shape, dtype) for shape, dtype in out_shapes]
    return pl.pallas_call(
        kernel,
        grid=(4,),
        in_specs=[block_spec(v, at in shared, last) for at, v in enumerate(inputs)],
        out_specs=[block_spec(v, at >= len(outs) - summed, last) for at, v in enumerate(outs)],
        out_shape=outs,
        scratch_shapes=[pltpu.VMEM((KEY, VAL), F32)],
        compiler_params=pltpu.CompilerParams(
            dimension_semantics=("arbitrary",), vmem_limit_bytes=56 * 2**20
        ),
    )(*inputs)


def by_slot(kernel, slotted, shared, order, out_shapes, summed=0):
    inputs = tuple(slotted) + tuple(shared)
    specs = [rows_spec(v) for v in slotted] + [rows_spec(v, True) for v in shared]
    outs = [jax.ShapeDtypeStruct(shape, dtype) for shape, dtype in out_shapes]
    out_specs = [rows_spec(v, at >= len(outs) - summed) for at, v in enumerate(outs)]
    return pl.pallas_call(
        kernel,
        grid=(4,),
        in_specs=[specs[at] for at in order],
        out_specs=out_specs,
        out_shape=outs,
        compiler_params=pltpu.CompilerParams(
            dimension_semantics=("arbitrary",), vmem_limit_bytes=56 * 2**20
        ),
    )(*[inputs[at] for at in order])


def slot_products(product, left, right):
    size = left.shape[0] // 4
    far = product(left[3 * size :], right).astype(BF16)
    left, right, far = lax.optimization_barrier((left, right, far))
    near = product(left[size : 3 * size], right)
    own = product(left[:size], right)
    return [own, near[:size], near[size:], far]


def place_columns(pieces, place, width):
    rows = pieces[0].shape[0]
    result = jnp.zeros((rows, 4 * width), F32)
    for slot, piece in enumerate(pieces):
        result = lax.dynamic_update_slice(result, piece.astype(F32), (0, (place ^ slot) * width))
    return result


def place_rows(pieces, place, height):
    result = jnp.zeros((4 * height, pieces[0].shape[1]), F32)
    for slot, piece in enumerate(pieces):
        result = lax.dynamic_update_slice(result, piece.astype(F32), ((place ^ slot) * height, 0))
    return result


def body(
    tokens,
    prescale,
    query_weight,
    key_weight,
    value_weight,
    gate_weight,
    groupscale,
    groupshift,
    output_weight,
    postscale,
    postshift,
    expand_weight,
    hiddenbias,
    reduce_weight,
    outputbias,
    cotangent,
    doc_lengths,
    segments,
):
    _, rows, width = tokens.shape
    half = rows // 2
    part = hiddenbias.shape[0] // 4
    core = lax.axis_index("head")
    place = lax.axis_index("batch")
    block = lax.axis_index("seq")
    within = lax.axis_size("seq") == 4
    size = half // 4

    def shares_of(*values):
        def share(of):
            cut = [lax.dynamic_slice_in_dim(v, (2 * of + core) * size, size, 0) for v in values]
            return jnp.concatenate(cut + [marks], axis=0)

        held = [share(place)]
        held += [swap_batch(share(place ^ slot), slot) for slot in (1, 2, 3)]
        return jnp.stack(held)

    def plane_of(held):
        result = jnp.zeros(held.shape, held.dtype)
        for steps in range(4):
            moved = lax.dynamic_index_in_dim(held, place ^ ((block + steps) % 4), 0, True)
            if steps:
                moved = turn(moved, steps)
            result = lax.dynamic_update_slice_in_dim(result, moved, (block - steps) % 4, 0)
        return result

    def give_back(value, dtype):
        if not within:
            return both_rows(value, swap_core(value)).astype(dtype)
        value = value.reshape(4, size, width)
        held = jnp.zeros((4, size, width), value.dtype)
        for steps in range(4):
            moved = lax.dynamic_index_in_dim(value, (block - steps) % 4, 0, True)
            if steps:
                moved = turn(moved, -steps)
            held = lax.dynamic_update_slice_in_dim(held, moved, (block + steps) % 4, 0)
        own = []
        for slot in range(4):
            moved = lax.dynamic_index_in_dim(held, place ^ slot, 0, False)
            own.append(swap_batch(moved, slot) if slot else moved)
        own = jnp.stack(own)
        far = swap_core(own)
        result = jnp.zeros((8, size, width), dtype)
        for slot in range(4):
            for side, shared in ((core, own), (1 - core, far)):
                result = lax.dynamic_update_slice_in_dim(
                    result, shared[slot : slot + 1].astype(dtype), 2 * (place ^ slot) + side, 0
                )
        return result.reshape(rows, width)

    def both_rows(own, far):
        result = jnp.zeros((rows, width), own.dtype)
        result = lax.dynamic_update_slice_in_dim(result, own, core * half, 0)
        return lax.dynamic_update_slice_in_dim(result, far, (1 - core) * half, 0)

    def cols_of(weight, size):
        return lax.dynamic_slice_in_dim(weight, place * size, size, 1)

    def rows_of(weight, size):
        return lax.dynamic_slice_in_dim(weight, place * size, size, 0)

    def gather_rows(weight):
        return lax.all_gather(weight, "seq", axis=0, tiled=True)

    def gather_cols(weight):
        return lax.all_gather(weight, "seq", axis=1, tiled=True)

    def scatter(grad, dimension):
        return lax.psum_scatter(grad.astype(BF16), "seq", scatter_dimension=dimension, tiled=True)

    project = jnp.concatenate(
        [
            cols_of(query_weight, KEY),
            cols_of(key_weight, KEY),
            cols_of(value_weight, VAL),
            cols_of(gate_weight, VAL),
        ],
        axis=1,
    )
    tokens = after(tokens, project)
    project = gather_rows(project)

    steps = jnp.arange(half, dtype=jnp.int32)
    if within:
        lengths = doc_lengths[0]
        marks = jnp.concatenate([segments[0], lengths // 64, lengths % 64]).astype(BF16)
        marks = jnp.pad(marks[None], ((0, 7), (0, width - marks.shape[0])))
        held = shares_of(cotangent[0], tokens[0])
        held_dy, held = held[:, :size], held[:, size:]
        held = plane_of(held)
        tokens_own = held[:, :size].reshape(half, width)
        marks = held[:, size].astype(jnp.int32)
        natural = marks[:, :rows]
        count = doc_lengths.shape[1]
        spans = marks[:, rows : rows + count] * 64 + marks[:, rows + count : rows + 2 * count]
        before = jnp.concatenate([jnp.full((1,), -1, jnp.int32), natural[:-1, rows - 1]])
        side, slot = jnp.arange(2)[:, None], jnp.arange(4)[None]
        share = 2 * (place ^ slot) + (core ^ side)
        index = share[:, :, None, None] * size + steps[:size]
        segment = jnp.take(natural.reshape(4, 8, size), share.reshape(8), axis=1)
        segment = segment.transpose(1, 0, 2).reshape(2, 4, 4, size)
        index = jnp.broadcast_to(index, segment.shape)
        at_block = jnp.arange(4)[None, None, :, None]
        stream_index = at_block * rows + index
        form = (1, 1, 4, 1)
    else:
        before = lax.ppermute(
            segments[0, rows - 1 :],
            "seq",
            [(source, source + 1) for source in range(lax.axis_size("seq") - 1)],
        )
        before = jnp.where(block == 0, -1, before)
        marks = jnp.concatenate([segments[0], doc_lengths[0], before])[None]
        marks = jnp.concatenate([marks, swap_batch(marks, 1)], axis=0)
        marks = jnp.concatenate([marks, swap_batch(marks, 2)], axis=0)
        natural, spans, before = marks[:, :rows], marks[:, rows:-1], marks[:, -1]
        tokens_own = lax.dynamic_slice_in_dim(tokens[0], core * half, half, 0)
        dy_own = lax.dynamic_slice_in_dim(cotangent[0], core * half, half, 0)
        index = jnp.stack([core * half + steps, (1 - core) * half + steps])[:, None]
        upper, lower = natural[None, :, :half], natural[None, :, half:]
        segment = jnp.where(
            core == 0,
            jnp.concatenate([upper, lower], axis=0),
            jnp.concatenate([lower, upper], axis=0),
        )
        index = jnp.broadcast_to(index, segment.shape)
        stream_index = block * rows + index
        form = (1, 4, 1)
    wide = tokens_own.astype(F32)
    inverse = lax.rsqrt(jnp.mean(wide * wide, axis=-1, keepdims=True) + 1e-06)
    scaled = wide * inverse
    normed_own = lax.optimization_barrier((scaled * prescale).astype(BF16))
    arrived = spread(normed_own)
    if within:
        dy_own = plane_of(after(held_dy, arrived[0])).reshape(half, width)
    normed = (normed_own,) + arrived
    normed = jnp.concatenate(normed + tuple(swap_core(piece) for piece in normed), axis=0)
    normed = lax.optimization_barrier(normed)
    dy_rows = jnp.concatenate((dy_own,) + spread(after(dy_own, arrived)), axis=0)
    output_own = gather_cols(after(rows_of(output_weight, VAL), arrived))
    expand_own = gather_rows(after(cols_of(expand_weight, part), normed))
    reduce_own = gather_cols(after(rows_of(reduce_weight, part), normed))

    last = natural[:, rows - 1]
    ends = jnp.cumsum(spans, axis=1).reshape(form + (-1,))
    spans = spans.reshape(form + (-1,))
    starts = jnp.sum(jnp.where(ends <= stream_index[..., None], spans, 0), axis=-1)
    positions = (stream_index - starts).astype(F32)
    middle = KEY // 2
    frequency = jnp.exp(-math.log(10000.0) * jnp.arange(middle, dtype=F32) / (middle - 1))
    phases = positions[..., None] * frequency
    cosine, sine = jnp.cos(phases), jnp.sin(phases)
    head = (core * 4 + place).astype(F32)
    log_rate = jnp.log1p(-jnp.exp2(-5.0 - head))
    entry = jnp.exp((index + 1).astype(F32) * log_rate) * (
        segment == before.reshape(form)
    ).astype(F32)
    exit_weight = jnp.exp((rows - 1 - index).astype(F32) * log_rate) * (
        segment == last.reshape(form)
    ).astype(F32)
    keep = jnp.exp(rows * log_rate) * (last == before).astype(F32)
    segment, index = segment.astype(F32), index.astype(F32)
    wide_keep = jnp.broadcast_to(keep.reshape(form), segment.shape)
    columns = jnp.stack([entry, exit_weight, segment, index, wide_keep], axis=-1)
    lines = jnp.stack([segment, index], axis=0)
    if within:
        lines = lines.transpose(3, 0, 1, 2, 4)
    else:
        lines = lines.transpose(2, 0, 1, 3)
    lines = lines.reshape(4, 2, rows)
    rate = jnp.full((1, 1), log_rate)
    cosine, sine, columns, lines = lax.optimization_barrier((cosine, sine, columns, lines))

    def rows_of_width(size, dtype=BF16):
        return (segment.shape + (size,), dtype)

    def entries(size, dtype=BF16):
        return ((4, KEY, size), dtype)

    scale_own = lax.dynamic_slice_in_dim(groupscale, place * VAL, VAL, 0)[None]
    shift_own = lax.dynamic_slice_in_dim(groupshift, place * VAL, VAL, 0)[None]
    normed_slots = normed.reshape(segment.shape + (width,))
    if within:
        queries, keys, values, memory, gate, unit, group_inverse, gated = by_block(
            stream_kernel,
            (normed_slots, project, cosine, sine, columns, lines, rate, scale_own, shift_own),
            (1, 6, 7, 8),
            (
                rows_of_width(KEY),
                rows_of_width(KEY),
                rows_of_width(VAL),
                entries(VAL),
                rows_of_width(VAL, F32),
                rows_of_width(VAL, F32),
                rows_of_width(1, F32),
                rows_of_width(VAL),
            ),
            False,
        )
    else:
        key_value = project[:, KEY : 2 * KEY + VAL]
        query_gate = jnp.concatenate([project[:, :KEY], project[:, 2 * KEY + VAL :]], axis=1)
        keys, values, added = by_slot(
            key_value_kernel,
            (normed_slots, cosine, sine, columns),
            (key_value,),
            (0, 4, 1, 2, 3),
            (rows_of_width(KEY), rows_of_width(VAL), entries(VAL, F32)),
        )
        memory = carry(keep, added, True)
        queries, gate, unit, group_inverse, gated = by_slot(
            retain_kernel,
            (normed_slots, cosine, sine, columns, lines, keys, values, memory),
            (query_gate, rate, scale_own, shift_own),
            (0, 8, 1, 2, 3, 4, 9, 5, 6, 7, 10, 11),
            (
                rows_of_width(KEY),
                rows_of_width(VAL, F32),
                rows_of_width(VAL, F32),
                rows_of_width(1, F32),
                rows_of_width(VAL),
            ),
        )
    gated_own = gated[0].reshape(4 * half, VAL)
    gated_far = swap_core(gated[1].reshape(4 * half, VAL))
    gated_both = jnp.concatenate([gated_own, gated_far], axis=-1)

    output_own = after(output_own, gated_both)
    output_both = jnp.concatenate([output_own, swap_core(output_own)], axis=0)
    bias_own = lax.dynamic_slice_in_dim(hiddenbias, place * part, part, 0)
    bias_both = jnp.concatenate([bias_own, swap_core(bias_own)], axis=0)

    branch = fold(slot_products(dot, gated_both, output_both))
    residual = wide + branch
    shifted = residual - jnp.mean(residual, axis=-1, keepdims=True)
    layer_inverse = lax.rsqrt(jnp.mean(shifted * shifted, axis=-1, keepdims=True) + 1e-05)
    standard = shifted * layer_inverse
    layered_own = (standard * postscale + postshift).astype(BF16)
    layered = jnp.concatenate((layered_own,) + spread(layered_own), axis=0)
    expand_own = after(expand_own, layered_own)
    expand_both = jnp.concatenate([expand_own, swap_core(expand_own)], axis=1)
    reduce_own = after(reduce_own, expand_own)
    reduce_both = jnp.concatenate([reduce_own, swap_core(reduce_own)], axis=0)

    hidden = dot(layered, expand_both) + bias_both
    cumulative = 0.5 * (1.0 + lax.erf(hidden * 0.5**0.5))
    active = (hidden * cumulative).astype(BF16)
    def core_sum(grad, dimension):
        size = grad.shape[dimension] // 2
        own = lax.slice_in_dim(grad, 0, size, axis=dimension)
        far = lax.slice_in_dim(grad, size, 2 * size, axis=dimension)
        return own + swap_core(far.astype(BF16)).astype(F32)

    dy_wide = dy_own.astype(F32)
    outputbias_grad = jnp.sum(dy_wide, axis=0)
    reduce_grad = scatter(core_sum(contract_rows(active, dy_rows), 0), 1)
    grad_active = contract_cols(dy_rows, reduce_both)
    slope = cumulative + hidden * jnp.exp(-0.5 * hidden * hidden) * (0.5 / math.pi) ** 0.5
    grad_hidden = (grad_active * slope).astype(BF16)
    hiddenbias_grad = jnp.sum(grad_hidden.astype(F32), axis=0)
    grad_layered = fold(slot_products(contract_cols, grad_hidden, expand_both))
    expand_grad = scatter(core_sum(contract_rows(layered, grad_hidden), 1), 0)
    postscale_grad = jnp.sum(grad_layered * standard, axis=0)
    postshift_grad = jnp.sum(grad_layered, axis=0)
    grad_residual = dy_wide + normalize_back(grad_layered * postscale, standard, layer_inverse)
    grad_branch_own = grad_residual.astype(BF16)
    grad_branch = jnp.concatenate((grad_branch_own,) + spread(grad_branch_own), axis=0)

    expanded = fold(slot_products(dot, after(active, grad_branch), reduce_both))
    output_rows = (residual + expanded + outputbias).astype(BF16)
    layer_output = give_back(output_rows, BF16)

    grad_gated_both = contract_cols(grad_branch, output_both).astype(BF16)
    grad_gated_own = grad_gated_both[:, :VAL].reshape(segment.shape[1:] + (VAL,))
    grad_gated_far = swap_core(grad_gated_both[:, VAL:]).reshape(segment.shape[1:] + (VAL,))
    output_grad = core_sum(contract_rows(gated_both, grad_branch), 0)
    if within:
        grads, group_sums = by_block(
            stream_back_kernel,
            (grad_gated_own, grad_gated_far, gate, unit, group_inverse, scale_own, shift_own)
            + (columns, lines, rate, cosine, sine, queries, keys, values, memory),
            (5, 6, 9),
            (rows_of_width(2 * KEY + 2 * VAL), ((2, VAL), F32)),
            True,
            summed=1,
        )
    else:
        grad_gate, grad_retained, reach, group_sums = by_slot(
            gate_back_kernel,
            (grad_gated_own, grad_gated_far, gate, unit, group_inverse, columns, queries),
            (scale_own, shift_own),
            (0, 1, 2, 3, 4, 7, 8, 5, 6),
            (rows_of_width(VAL), rows_of_width(VAL), entries(VAL, F32), ((2, VAL), F32)),
            summed=1,
        )
        grad_memory = carry(keep, reach, False)
        grad_query_gate, grad_keys, grad_values = by_slot(
            local_back_kernel,
            (grad_retained, grad_gate, queries, keys, values, memory, columns, lines)
            + (cosine, sine),
            (rate,),
            (0, 1, 2, 3, 4, 5, 6, 7, 10, 8, 9),
            (rows_of_width(KEY + VAL), rows_of_width(KEY, F32), rows_of_width(VAL, F32)),
        )
        (grad_key_value,) = by_slot(
            state_back_kernel,
            (grad_keys, grad_values, keys, values, grad_memory, columns, cosine, sine),
            (),
            range(8),
            (rows_of_width(KEY + VAL),),
        )
        grads = jnp.concatenate(
            [grad_query_gate[..., :KEY], grad_key_value, grad_query_gate[..., KEY:]], axis=-1
        )
    groupscale_grad, groupshift_grad = group_sums[0], group_sums[1]
    grads = grads.reshape(4 * rows, 2 * KEY + 2 * VAL)
    gate_grad = contract_rows(normed, grads[:, 2 * KEY + VAL :]).astype(BF16)
    first_grad = contract_rows(normed, grads[:, : 2 * KEY + VAL]).astype(BF16)
    grads = after(grads, gate_grad, first_grad)
    far_terms = contract_cols(grads[4 * half :], project).astype(BF16)
    far_terms = swap_core(far_terms).astype(F32)
    far_corner = contract_cols(grads[3 * half : 4 * half], project) + far_terms[3 * half :]
    own_terms = contract_cols(grads[: 3 * half], project) + far_terms[: 3 * half]
    own_terms = [own_terms[slot * half : (slot + 1) * half] for slot in range(3)]
    grad_normed = fold(own_terms + [far_corner.astype(BF16)])
    output_grad = scatter(output_grad, 1)
    gate_grad = scatter(gate_grad, 0)
    first_grad = scatter(first_grad, 0)
    prescale_grad = jnp.sum(grad_normed * scaled, axis=0)
    grad_scaled = grad_normed * prescale
    grad_rows = grad_residual + inverse * (
        grad_scaled - scaled * jnp.mean(grad_scaled * scaled, axis=-1, keepdims=True)
    )
    tokens_grad = give_back(grad_rows.astype(BF16) if within else grad_rows, F32)

    by_width = [prescale_grad, postscale_grad, postshift_grad, outputbias_grad]
    over_cores = swap_core(jnp.concatenate([hiddenbias_grad[part:]] + by_width))
    over_cores = over_cores + jnp.concatenate([hiddenbias_grad[:part]] + by_width)
    spaced = [
        lax.dynamic_update_slice(jnp.zeros((4 * part,), F32), piece, (place * part,))
        for piece in (over_cores[:part], groupscale_grad, groupshift_grad)
    ]
    sums = total(jnp.concatenate([over_cores[part:]] + spaced))
    cuts = [width * at for at in range(1, 5)] + [4 * width + 4 * part, 4 * width + 8 * part]
    prescale_sum, postscale_sum, postshift_sum, outputbias_sum, hiddenbias_sum, scale_sum, shift_sum = (
        jnp.split(sums, cuts)
    )

    def all_pieces(grad):
        return (grad,) + spread(grad)

    reduce_pieces = all_pieces(reduce_grad)
    expand_pieces = all_pieces(expand_grad)
    output_pieces = all_pieces(output_grad)
    gate_pieces = all_pieces(gate_grad)
    first_pieces = all_pieces(first_grad)
    return (
        layer_output[None],
        tokens_grad[None],
        prescale_sum,
        place_columns([piece[:, :KEY] for piece in first_pieces], place, KEY),
        place_columns([piece[:, KEY : 2 * KEY] for piece in first_pieces], place, KEY),
        place_columns([piece[:, 2 * KEY :] for piece in first_pieces], place, VAL),
        place_columns(gate_pieces, place, VAL),
        scale_sum,
        shift_sum,
        place_rows(output_pieces, place, VAL),
        postscale_sum,
        postshift_sum,
        place_columns(expand_pieces, place, part),
        hiddenbias_sum,
        place_rows(reduce_pieces, place, part),
        outputbias_sum,
    )


def solution(mesh):
    in_specs = (
        P("batch", "seq", None),
        P(),
        P("seq", "head"),
        P("seq", "head"),
        P("seq", "head"),
        P("seq", "head"),
        P("head"),
        P("head"),
        P("head", "seq"),
        P(),
        P(),
        P("seq", "head"),
        P("head"),
        P("head", "seq"),
        P(),
        P("batch", "seq", None),
        P("batch", None),
        P("batch", "seq"),
    )
    out_specs = (
        P("batch", "seq", None),
        P("batch", "seq", None),
        P(),
        P("seq", "head"),
        P("seq", "head"),
        P("seq", "head"),
        P("seq", "head"),
        P("head"),
        P("head"),
        P("head", "seq"),
        P(),
        P(),
        P("seq", "head"),
        P("head"),
        P("head", "seq"),
        P(),
    )
    return jax.shard_map(body, mesh=mesh, in_specs=in_specs, out_specs=out_specs, check_vma=False)
```

```python
import math

import jax
import jax.numpy as jnp
from jax import lax
from jax.experimental import pallas as pl
from jax.experimental.pallas import tpu as pltpu
from jax.sharding import PartitionSpec as P

KEY = 256
VAL = 512
F32 = jnp.float32
BF16 = jnp.bfloat16


def swap_core(value):
    return lax.ppermute(value, "head", [(0, 1), (1, 0)])


def swap_batch(value, mask):
    return lax.ppermute(value, "batch", [(place, place ^ mask) for place in range(4)])


def after(value, *earlier):
    return lax.optimization_barrier((value,) + earlier)[0]


def spread(piece):
    return relay(swap_batch(piece, 1), swap_batch(piece, 2))


def relay(first, second):
    middle = first.shape[0] // 2
    upper = swap_batch(first[:middle], 2)
    lower = swap_batch(second[middle:], 1)
    return first, second, jnp.concatenate([upper, lower], axis=0)


def fold(parts):
    middle = parts[3].shape[0] // 2
    far = parts[3]
    upper = swap_batch(far[:middle], 1)
    lower = swap_batch(far[middle:], 2)
    to_first = jnp.concatenate(
        [parts[1][:middle], parts[1][middle:] + lower.astype(F32)], axis=0
    ).astype(BF16)
    to_second = jnp.concatenate(
        [parts[2][:middle] + upper.astype(F32), parts[2][middle:]], axis=0
    ).astype(BF16)
    first = swap_batch(to_first, 1)
    second = swap_batch(to_second, 2)
    return parts[0] + first.astype(F32) + second.astype(F32)


def total(value):
    for axis in ("batch", "seq"):
        count = lax.axis_size(axis)
        step = 1
        while step < count:
            moved = lax.ppermute(value, axis, [(place, place ^ step) for place in range(count)])
            value = value + moved
            step *= 2
    return value


def turn(value, steps):
    count = lax.axis_size("seq")
    return lax.ppermute(
        value, "seq", [(source, (source + steps) % count) for source in range(count)]
    )


def hop(value, source, target):
    return lax.ppermute(value, "seq", [(source, target)])


def carry(keep, added, forward):
    count = lax.axis_size("seq")
    entered = []
    for chunk in range(0, 4, 2):
        factor = keep[chunk : chunk + 2, None, None]
        own = added[chunk : chunk + 2]
        state = jnp.zeros(own.shape, BF16)
        for step in range(count - 1):
            sent = (factor * state.astype(F32) + own).astype(BF16)
            source, target = (step, step + 1) if forward else (count - 1 - step, count - 2 - step)
            state = state + hop(sent, source, target)
        entered.append(state)
    return jnp.concatenate(entered, axis=0)


def dot(left, right):
    return jnp.dot(left, right, preferred_element_type=F32)


def contract_rows(left, right):
    return lax.dot_general(left, right, (((0,), (0,)), ((), ())), preferred_element_type=F32)


def contract_cols(left, right):
    return lax.dot_general(left, right, (((1,), (1,)), ((), ())), preferred_element_type=F32)


def normalize_back(grad_unit, unit_norm, inverse):
    mean_grad = jnp.mean(grad_unit, axis=-1, keepdims=True)
    mean_cross = jnp.mean(grad_unit * unit_norm, axis=-1, keepdims=True)
    return inverse * (grad_unit - mean_grad - unit_norm * mean_cross)


def rotated(values, cosine, sine):
    middle = values.shape[-1] // 2
    former, latter = (values[:, :middle], values[:, middle:])
    return jnp.concatenate(
        [former * cosine - latter * sine, latter * cosine + former * sine], axis=-1
    )


def flat(ref):
    value = ref[...]
    return value.reshape(-1, value.shape[-1])


def put(ref, value):
    ref[...] = value.reshape(ref.shape).astype(ref.dtype)


def weigh(value, weight):
    return (value.astype(F32) * weight).astype(BF16)


def decay_of(columns, lines, rate):
    distance = columns[:, 3:4] - lines[1:2]
    linked = (columns[:, 2:3] == lines[0:1]) & (distance >= 0)
    return jnp.where(linked, jnp.exp(jnp.maximum(distance, 0.0) * rate), 0.0)


def key_value_kernel(normed, weight, cosine, sine, columns, keys, values, added):
    product = dot(flat(normed), weight[...])
    key = (rotated(product[:, :KEY], flat(cosine), flat(sine)) * KEY ** (-0.5)).astype(BF16)
    value = product[:, KEY:].astype(BF16)
    put(keys, key)
    put(values, value)
    put(added, contract_rows(weigh(key, flat(columns)[:, 1:2]), value))


def retain_kernel(
    normed, weight, cosine, sine, columns, lines, rate, keys, values, memory, scale, shift,
    queries, gate, unit, inverse, gated,
):
    product = dot(flat(normed), weight[...])
    query = rotated(product[:, :KEY], flat(cosine), flat(sine)).astype(BF16)
    table = flat(columns)
    decay = decay_of(table, flat(lines), rate[...])
    mixing = (contract_cols(query, flat(keys)) * decay).astype(BF16)
    retained = dot(mixing, flat(values)) + dot(weigh(query, table[:, 0:1]), flat(memory))
    centred = retained - jnp.mean(retained, axis=-1, keepdims=True)
    factor = lax.rsqrt(jnp.mean(centred * centred, axis=-1, keepdims=True) + 1.0)
    unit_norm = centred * factor
    gate_pre = product[:, KEY:]
    put(queries, query)
    put(gate, gate_pre)
    put(unit, unit_norm)
    put(inverse, factor)
    grouped = unit_norm * scale[...] + shift[...]
    put(gated, gate_pre * jax.nn.sigmoid(gate_pre) * grouped)


def gate_back_kernel(
    grad_own, grad_far, gate, unit, inverse, scale, shift, columns, queries,
    grad_gate, grad_retained, reach, sums,
):
    grad_gated = jnp.concatenate([flat(grad_own), flat(grad_far)], axis=0).astype(F32)
    gate_pre, unit_norm = flat(gate), flat(unit)
    grouped = unit_norm * scale[...] + shift[...]
    sigmoid = jax.nn.sigmoid(gate_pre)
    put(grad_gate, grad_gated * grouped * sigmoid * (1.0 + gate_pre * (1.0 - sigmoid)))
    grad_grouped = grad_gated * (gate_pre * sigmoid)
    part = jnp.concatenate(
        [
            jnp.sum(grad_grouped * unit_norm, axis=0, keepdims=True),
            jnp.sum(grad_grouped, axis=0, keepdims=True),
        ],
        axis=0,
    )

    @pl.when(pl.program_id(0) == 0)
    def first():
        sums[...] = part

    @pl.when(pl.program_id(0) > 0)
    def later():
        sums[...] += part

    grad = normalize_back(grad_grouped * scale[...], unit_norm, flat(inverse)).astype(BF16)
    put(grad_retained, grad)
    put(reach, contract_rows(weigh(flat(queries), flat(columns)[:, 0:1]), grad))


def local_back_kernel(
    grad_retained, grad_gate, queries, keys, values, memory, columns, lines, rate, cosine, sine,
    grad_query_gate, grad_keys, grad_values,
):
    grad, query, key, value = flat(grad_retained), flat(queries), flat(keys), flat(values)
    table = flat(columns)
    decay = decay_of(table, flat(lines), rate[...])
    mixing = (contract_cols(query, key) * decay).astype(BF16)
    grad_scores = (contract_cols(grad, value) * decay).astype(BF16)
    grad_query = dot(grad_scores, key) + table[:, 0:1] * contract_cols(grad, flat(memory))
    grad_query = rotated(grad_query, flat(cosine), -flat(sine)).astype(BF16)
    put(grad_query_gate, jnp.concatenate([grad_query, flat(grad_gate)], axis=-1))
    put(grad_keys, contract_rows(grad_scores, query))
    put(grad_values, contract_rows(mixing, grad))


def state_back_kernel(
    grad_keys, grad_values, keys, values, grad_memory, columns, cosine, sine, grad_key_value
):
    weight = flat(columns)[:, 1:2]
    state = flat(grad_memory)
    grad_key = flat(grad_keys) + weight * contract_cols(flat(values), state)
    grad_key = rotated(grad_key, flat(cosine), -flat(sine)) * KEY ** (-0.5)
    grad_value = flat(grad_values) + dot(weigh(flat(keys), weight), state)
    put(
        grad_key_value,
        jnp.concatenate([grad_key.astype(BF16), grad_value.astype(BF16)], axis=-1),
    )


def stream_kernel(
    normed, weight, cosine, sine, columns, lines, rate, scale, shift,
    queries, keys, values, memory, gate, unit, inverse, gated, state,
):
    @pl.when(pl.program_id(0) == 0)
    def first():
        state[...] = jnp.zeros_like(state)

    product = dot(flat(normed), weight[...])
    table = flat(columns)
    query = rotated(product[:, :KEY], flat(cosine), flat(sine)).astype(BF16)
    key = rotated(product[:, KEY : 2 * KEY], flat(cosine), flat(sine)) * KEY ** (-0.5)
    key = key.astype(BF16)
    value = product[:, 2 * KEY : 2 * KEY + VAL].astype(BF16)
    gate_pre = product[:, 2 * KEY + VAL :]
    low = state[...].astype(BF16)
    decay = decay_of(table, flat(lines), rate[...])
    mixing = (contract_cols(query, key) * decay).astype(BF16)
    retained = dot(mixing, value) + dot(weigh(query, table[:, 0:1]), low)
    state[...] = table[0:1, 4:5] * state[...] + contract_rows(weigh(key, table[:, 1:2]), value)
    centred = retained - jnp.mean(retained, axis=-1, keepdims=True)
    factor = lax.rsqrt(jnp.mean(centred * centred, axis=-1, keepdims=True) + 1.0)
    unit_norm = centred * factor
    put(queries, query)
    put(keys, key)
    put(values, value)
    put(memory, low)
    put(gate, gate_pre)
    put(unit, unit_norm)
    put(inverse, factor)
    grouped = unit_norm * scale[...] + shift[...]
    put(gated, gate_pre * jax.nn.sigmoid(gate_pre) * grouped)


def stream_back_kernel(
    grad_own, grad_far, gate, unit, inverse, scale, shift, columns, lines, rate, cosine, sine,
    queries, keys, values, memory, grads, sums, state,
):
    grad_gated = jnp.concatenate([flat(grad_own), flat(grad_far)], axis=0).astype(F32)
    gate_pre, unit_norm, table = flat(gate), flat(unit), flat(columns)
    query, key, value = flat(queries), flat(keys), flat(values)
    entry, weight = table[:, 0:1], table[:, 1:2]
    grouped = unit_norm * scale[...] + shift[...]
    sigmoid = jax.nn.sigmoid(gate_pre)
    grad_gate = grad_gated * grouped * sigmoid * (1.0 + gate_pre * (1.0 - sigmoid))
    grad_grouped = grad_gated * (gate_pre * sigmoid)

    @pl.when(pl.program_id(0) == 0)
    def first():
        state[...] = jnp.zeros_like(state)
        sums[...] = jnp.zeros_like(sums)

    sums[0:1] += jnp.sum(grad_grouped * unit_norm, axis=0, keepdims=True)
    sums[1:2] += jnp.sum(grad_grouped, axis=0, keepdims=True)
    grad = normalize_back(grad_grouped * scale[...], unit_norm, flat(inverse)).astype(BF16)
    decay = decay_of(table, flat(lines), rate[...])
    mixing = (contract_cols(query, key) * decay).astype(BF16)
    grad_scores = (contract_cols(grad, value) * decay).astype(BF16)
    low = state[...].astype(BF16)
    grad_query = dot(grad_scores, key) + entry * contract_cols(grad, flat(memory))
    grad_key = contract_rows(grad_scores, query) + weight * contract_cols(value, low)
    grad_value = contract_rows(mixing, grad) + dot(weigh(key, weight), low)
    state[...] = table[0:1, 4:5] * state[...] + contract_rows(weigh(query, entry), grad)
    cosines, sines = flat(cosine), -flat(sine)
    put(
        grads,
        jnp.concatenate(
            [
                rotated(grad_query, cosines, sines).astype(BF16),
                (rotated(grad_key, cosines, sines) * KEY ** (-0.5)).astype(BF16),
                grad_value.astype(BF16),
                grad_gate.astype(BF16),
            ],
            axis=-1,
        ),
    )


def rows_spec(value, whole=False):
    if whole:
        return pl.BlockSpec(value.shape, lambda slot: (0,) * len(value.shape))
    if len(value.shape) == 4:
        two, _, half, width = value.shape
        return pl.BlockSpec((two, 1, half, width), lambda slot: (0, slot, 0, 0))
    return pl.BlockSpec((1,) + value.shape[1:], lambda slot: (slot, 0, 0))


def block_spec(value, whole=False, last=False):
    if whole:
        return pl.BlockSpec(value.shape, lambda step: (0,) * len(value.shape))
    rank = len(value.shape)
    shape = value.shape[: rank - 3] + (1,) + value.shape[rank - 2 :]
    return pl.BlockSpec(
        shape, lambda step: (0,) * (rank - 3) + (3 - step if last else step,) + (0, 0)
    )


def by_block(kernel, inputs, shared, out_shapes, last, summed=0):
    outs = [jax.ShapeDtypeStruct(shape, dtype) for shape, dtype in out_shapes]
    return pl.pallas_call(
        kernel,
        grid=(4,),
        in_specs=[block_spec(v, at in shared, last) for at, v in enumerate(inputs)],
        out_specs=[block_spec(v, at >= len(outs) - summed, last) for at, v in enumerate(outs)],
        out_shape=outs,
        scratch_shapes=[pltpu.VMEM((KEY, VAL), F32)],
        compiler_params=pltpu.CompilerParams(
            dimension_semantics=("arbitrary",), vmem_limit_bytes=56 * 2**20
        ),
    )(*inputs)


def by_slot(kernel, slotted, shared, order, out_shapes, summed=0):
    inputs = tuple(slotted) + tuple(shared)
    specs = [rows_spec(v) for v in slotted] + [rows_spec(v, True) for v in shared]
    outs = [jax.ShapeDtypeStruct(shape, dtype) for shape, dtype in out_shapes]
    out_specs = [rows_spec(v, at >= len(outs) - summed) for at, v in enumerate(outs)]
    return pl.pallas_call(
        kernel,
        grid=(4,),
        in_specs=[specs[at] for at in order],
        out_specs=out_specs,
        out_shape=outs,
        compiler_params=pltpu.CompilerParams(
            dimension_semantics=("arbitrary",), vmem_limit_bytes=56 * 2**20
        ),
    )(*[inputs[at] for at in order])


def slot_products(product, left, right):
    size = left.shape[0] // 4
    far = product(left[3 * size :], right).astype(BF16)
    left, right, far = lax.optimization_barrier((left, right, far))
    near = product(left[size : 3 * size], right)
    own = product(left[:size], right)
    return [own, near[:size], near[size:], far]


def place_columns(pieces, place, width):
    rows = pieces[0].shape[0]
    result = jnp.zeros((rows, 4 * width), F32)
    for slot, piece in enumerate(pieces):
        result = lax.dynamic_update_slice(result, piece.astype(F32), (0, (place ^ slot) * width))
    return result


def place_rows(pieces, place, height):
    result = jnp.zeros((4 * height, pieces[0].shape[1]), F32)
    for slot, piece in enumerate(pieces):
        result = lax.dynamic_update_slice(result, piece.astype(F32), ((place ^ slot) * height, 0))
    return result


def body(
    tokens,
    prescale,
    query_weight,
    key_weight,
    value_weight,
    gate_weight,
    groupscale,
    groupshift,
    output_weight,
    postscale,
    postshift,
    expand_weight,
    hiddenbias,
    reduce_weight,
    outputbias,
    cotangent,
    doc_lengths,
    segments,
):
    _, rows, width = tokens.shape
    half = rows // 2
    part = hiddenbias.shape[0] // 4
    core = lax.axis_index("head")
    place = lax.axis_index("batch")
    block = lax.axis_index("seq")
    within = lax.axis_size("seq") == 4
    size = half // 4

    def shares_of(*values):
        def share(of):
            cut = [lax.dynamic_slice_in_dim(v, (2 * of + core) * size, size, 0) for v in values]
            return jnp.concatenate(cut + [marks], axis=0)

        held = [share(place)]
        held += [swap_batch(share(place ^ slot), slot) for slot in (1, 2, 3)]
        return jnp.stack(held)

    def plane_of(held):
        result = jnp.zeros(held.shape, held.dtype)
        for steps in range(4):
            moved = lax.dynamic_index_in_dim(held, place ^ ((block + steps) % 4), 0, True)
            if steps:
                moved = turn(moved, steps)
            result = lax.dynamic_update_slice_in_dim(result, moved, (block - steps) % 4, 0)
        return result

    def send_back(value):
        value = value.reshape(4, size, width)
        parts = [
            lax.dynamic_index_in_dim(value, (block - steps) % 4, 0, True) for steps in range(4)
        ]
        return parts[:1] + [turn(parts[steps], -steps) for steps in (1, 2, 3)]

    def place_back(parts, dtype):
        held = jnp.zeros((4, size, width), parts[0].dtype)
        for steps, part in enumerate(parts):
            held = lax.dynamic_update_slice_in_dim(held, part, (block + steps) % 4, 0)
        own = []
        for slot in range(4):
            moved = lax.dynamic_index_in_dim(held, place ^ slot, 0, False)
            own.append(swap_batch(moved, slot) if slot else moved)
        own = jnp.stack(own)
        far = swap_core(own)
        result = jnp.zeros((8, size, width), dtype)
        for slot in range(4):
            for side, shared in ((core, own), (1 - core, far)):
                result = lax.dynamic_update_slice_in_dim(
                    result, shared[slot : slot + 1].astype(dtype), 2 * (place ^ slot) + side, 0
                )
        return result.reshape(rows, width)

    def both_rows(own, far):
        result = jnp.zeros((rows, width), own.dtype)
        result = lax.dynamic_update_slice_in_dim(result, own, core * half, 0)
        return lax.dynamic_update_slice_in_dim(result, far, (1 - core) * half, 0)

    def cols_of(weight, size):
        return lax.dynamic_slice_in_dim(weight, place * size, size, 1)

    def rows_of(weight, size):
        return lax.dynamic_slice_in_dim(weight, place * size, size, 0)

    def gather_rows(weight):
        return lax.all_gather(weight, "seq", axis=0, tiled=True)

    def gather_cols(weight):
        return lax.all_gather(weight, "seq", axis=1, tiled=True)

    def scatter(grad, dimension):
        return lax.psum_scatter(grad.astype(BF16), "seq", scatter_dimension=dimension, tiled=True)

    project = jnp.concatenate(
        [
            cols_of(query_weight, KEY),
            cols_of(key_weight, KEY),
            cols_of(value_weight, VAL),
            cols_of(gate_weight, VAL),
        ],
        axis=1,
    )
    tokens = after(tokens, project)
    project = gather_rows(project)

    steps = jnp.arange(half, dtype=jnp.int32)
    if within:
        lengths = doc_lengths[0]
        marks = jnp.concatenate([segments[0], lengths // 64, lengths % 64]).astype(BF16)
        marks = jnp.pad(marks[None], ((0, 7), (0, width - marks.shape[0])))
        held = shares_of(cotangent[0], tokens[0])
        held_dy, held = held[:, :size], held[:, size:]
        held = plane_of(held)
        tokens_own = held[:, :size].reshape(half, width)
        marks = held[:, size].astype(jnp.int32)
        natural = marks[:, :rows]
        count = doc_lengths.shape[1]
        spans = marks[:, rows : rows + count] * 64 + marks[:, rows + count : rows + 2 * count]
        before = jnp.concatenate([jnp.full((1,), -1, jnp.int32), natural[:-1, rows - 1]])
        side, slot = jnp.arange(2)[:, None], jnp.arange(4)[None]
        share = 2 * (place ^ slot) + (core ^ side)
        index = share[:, :, None, None] * size + steps[:size]
        segment = jnp.take(natural.reshape(4, 8, size), share.reshape(8), axis=1)
        segment = segment.transpose(1, 0, 2).reshape(2, 4, 4, size)
        index = jnp.broadcast_to(index, segment.shape)
        at_block = jnp.arange(4)[None, None, :, None]
        stream_index = at_block * rows + index
        form = (1, 1, 4, 1)
    else:
        before = lax.ppermute(
            segments[0, rows - 1 :],
            "seq",
            [(source, source + 1) for source in range(lax.axis_size("seq") - 1)],
        )
        before = jnp.where(block == 0, -1, before)
        marks = jnp.concatenate([segments[0], doc_lengths[0], before])[None]
        marks = jnp.concatenate([marks, swap_batch(marks, 1)], axis=0)
        marks = jnp.concatenate([marks, swap_batch(marks, 2)], axis=0)
        natural, spans, before = marks[:, :rows], marks[:, rows:-1], marks[:, -1]
        tokens_own = lax.dynamic_slice_in_dim(tokens[0], core * half, half, 0)
        dy_own = lax.dynamic_slice_in_dim(cotangent[0], core * half, half, 0)
        index = jnp.stack([core * half + steps, (1 - core) * half + steps])[:, None]
        upper, lower = natural[None, :, :half], natural[None, :, half:]
        segment = jnp.where(
            core == 0,
            jnp.concatenate([upper, lower], axis=0),
            jnp.concatenate([lower, upper], axis=0),
        )
        index = jnp.broadcast_to(index, segment.shape)
        stream_index = block * rows + index
        form = (1, 4, 1)
    wide = tokens_own.astype(F32)
    inverse = lax.rsqrt(jnp.mean(wide * wide, axis=-1, keepdims=True) + 1e-06)
    scaled = wide * inverse
    normed_own = lax.optimization_barrier((scaled * prescale).astype(BF16))
    arrived = spread(normed_own)
    if within:
        dy_own = plane_of(after(held_dy, arrived[0])).reshape(half, width)
    normed = (normed_own,) + arrived
    normed = jnp.concatenate(normed + tuple(swap_core(piece) for piece in normed), axis=0)
    normed = lax.optimization_barrier(normed)
    dy_rows = jnp.concatenate((dy_own,) + spread(after(dy_own, arrived)), axis=0)
    output_own = gather_cols(after(rows_of(output_weight, VAL), arrived))
    expand_own = gather_rows(after(cols_of(expand_weight, part), normed))
    reduce_own = gather_cols(after(rows_of(reduce_weight, part), normed))

    last = natural[:, rows - 1]
    ends = jnp.cumsum(spans, axis=1).reshape(form + (-1,))
    spans = spans.reshape(form + (-1,))
    starts = jnp.sum(jnp.where(ends <= stream_index[..., None], spans, 0), axis=-1)
    positions = (stream_index - starts).astype(F32)
    middle = KEY // 2
    frequency = jnp.exp(-math.log(10000.0) * jnp.arange(middle, dtype=F32) / (middle - 1))
    phases = positions[..., None] * frequency
    cosine, sine = jnp.cos(phases), jnp.sin(phases)
    head = (core * 4 + place).astype(F32)
    log_rate = jnp.log1p(-jnp.exp2(-5.0 - head))
    entry = jnp.exp((index + 1).astype(F32) * log_rate) * (
        segment == before.reshape(form)
    ).astype(F32)
    exit_weight = jnp.exp((rows - 1 - index).astype(F32) * log_rate) * (
        segment == last.reshape(form)
    ).astype(F32)
    keep = jnp.exp(rows * log_rate) * (last == before).astype(F32)
    segment, index = segment.astype(F32), index.astype(F32)
    wide_keep = jnp.broadcast_to(keep.reshape(form), segment.shape)
    columns = jnp.stack([entry, exit_weight, segment, index, wide_keep], axis=-1)
    lines = jnp.stack([segment, index], axis=0)
    if within:
        lines = lines.transpose(3, 0, 1, 2, 4)
    else:
        lines = lines.transpose(2, 0, 1, 3)
    lines = lines.reshape(4, 2, rows)
    rate = jnp.full((1, 1), log_rate)
    cosine, sine, columns, lines = lax.optimization_barrier((cosine, sine, columns, lines))

    def rows_of_width(size, dtype=BF16):
        return (segment.shape + (size,), dtype)

    def entries(size, dtype=BF16):
        return ((4, KEY, size), dtype)

    scale_own = lax.dynamic_slice_in_dim(groupscale, place * VAL, VAL, 0)[None]
    shift_own = lax.dynamic_slice_in_dim(groupshift, place * VAL, VAL, 0)[None]
    normed_slots = normed.reshape(segment.shape + (width,))
    if within:
        queries, keys, values, memory, gate, unit, group_inverse, gated = by_block(
            stream_kernel,
            (normed_slots, project, cosine, sine, columns, lines, rate, scale_own, shift_own),
            (1, 6, 7, 8),
            (
                rows_of_width(KEY),
                rows_of_width(KEY),
                rows_of_width(VAL),
                entries(VAL),
                rows_of_width(VAL, F32),
                rows_of_width(VAL, F32),
                rows_of_width(1, F32),
                rows_of_width(VAL),
            ),
            False,
        )
    else:
        key_value = project[:, KEY : 2 * KEY + VAL]
        query_gate = jnp.concatenate([project[:, :KEY], project[:, 2 * KEY + VAL :]], axis=1)
        keys, values, added = by_slot(
            key_value_kernel,
            (normed_slots, cosine, sine, columns),
            (key_value,),
            (0, 4, 1, 2, 3),
            (rows_of_width(KEY), rows_of_width(VAL), entries(VAL, F32)),
        )
        memory = carry(keep, added, True)
        queries, gate, unit, group_inverse, gated = by_slot(
            retain_kernel,
            (normed_slots, cosine, sine, columns, lines, keys, values, memory),
            (query_gate, rate, scale_own, shift_own),
            (0, 8, 1, 2, 3, 4, 9, 5, 6, 7, 10, 11),
            (
                rows_of_width(KEY),
                rows_of_width(VAL, F32),
                rows_of_width(VAL, F32),
                rows_of_width(1, F32),
                rows_of_width(VAL),
            ),
        )
    gated_own = gated[0].reshape(4 * half, VAL)
    gated_far = swap_core(gated[1].reshape(4 * half, VAL))
    gated_both = jnp.concatenate([gated_own, gated_far], axis=-1)

    output_own = after(output_own, gated_both)
    output_both = jnp.concatenate([output_own, swap_core(output_own)], axis=0)
    bias_own = lax.dynamic_slice_in_dim(hiddenbias, place * part, part, 0)
    bias_both = jnp.concatenate([bias_own, swap_core(bias_own)], axis=0)

    branch = fold(slot_products(dot, gated_both, output_both))
    residual = wide + branch
    shifted = residual - jnp.mean(residual, axis=-1, keepdims=True)
    layer_inverse = lax.rsqrt(jnp.mean(shifted * shifted, axis=-1, keepdims=True) + 1e-05)
    standard = shifted * layer_inverse
    layered_own = (standard * postscale + postshift).astype(BF16)
    layered = jnp.concatenate((layered_own,) + spread(layered_own), axis=0)
    expand_own = after(expand_own, layered_own)
    expand_both = jnp.concatenate([expand_own, swap_core(expand_own)], axis=1)
    reduce_own = after(reduce_own, expand_own)
    reduce_both = jnp.concatenate([reduce_own, swap_core(reduce_own)], axis=0)

    hidden = dot(layered, expand_both) + bias_both
    cumulative = 0.5 * (1.0 + lax.erf(hidden * 0.5**0.5))
    active = (hidden * cumulative).astype(BF16)
    def core_sum(grad, dimension):
        size = grad.shape[dimension] // 2
        own = lax.slice_in_dim(grad, 0, size, axis=dimension)
        far = lax.slice_in_dim(grad, size, 2 * size, axis=dimension)
        return own + swap_core(far.astype(BF16)).astype(F32)

    dy_wide = dy_own.astype(F32)
    outputbias_grad = jnp.sum(dy_wide, axis=0)
    reduce_grad = scatter(core_sum(contract_rows(active, dy_rows), 0), 1)
    grad_active = contract_cols(dy_rows, reduce_both)
    slope = cumulative + hidden * jnp.exp(-0.5 * hidden * hidden) * (0.5 / math.pi) ** 0.5
    grad_hidden = (grad_active * slope).astype(BF16)
    hiddenbias_grad = jnp.sum(grad_hidden.astype(F32), axis=0)
    grad_layered = fold(slot_products(contract_cols, grad_hidden, expand_both))
    expand_grad = scatter(core_sum(contract_rows(layered, grad_hidden), 1), 0)
    postscale_grad = jnp.sum(grad_layered * standard, axis=0)
    postshift_grad = jnp.sum(grad_layered, axis=0)
    grad_residual = dy_wide + normalize_back(grad_layered * postscale, standard, layer_inverse)
    grad_branch_own = grad_residual.astype(BF16)
    grad_branch = jnp.concatenate((grad_branch_own,) + spread(grad_branch_own), axis=0)

    expanded = fold(slot_products(dot, after(active, grad_branch), reduce_both))
    output_rows = (residual + expanded + outputbias).astype(BF16)
    if within:
        layer_output = place_back(send_back(output_rows), BF16)
    else:
        layer_output = both_rows(output_rows, swap_core(output_rows))

    grad_gated_both = contract_cols(grad_branch, output_both).astype(BF16)
    grad_gated_own = grad_gated_both[:, :VAL].reshape(segment.shape[1:] + (VAL,))
    grad_gated_far = swap_core(grad_gated_both[:, VAL:]).reshape(segment.shape[1:] + (VAL,))
    output_grad = core_sum(contract_rows(gated_both, grad_branch), 0)
    if within:
        grads, group_sums = by_block(
            stream_back_kernel,
            (grad_gated_own, grad_gated_far, gate, unit, group_inverse, scale_own, shift_own)
            + (columns, lines, rate, cosine, sine, queries, keys, values, memory),
            (5, 6, 9),
            (rows_of_width(2 * KEY + 2 * VAL), ((2, VAL), F32)),
            True,
            summed=1,
        )
    else:
        grad_gate, grad_retained, reach, group_sums = by_slot(
            gate_back_kernel,
            (grad_gated_own, grad_gated_far, gate, unit, group_inverse, columns, queries),
            (scale_own, shift_own),
            (0, 1, 2, 3, 4, 7, 8, 5, 6),
            (rows_of_width(VAL), rows_of_width(VAL), entries(VAL, F32), ((2, VAL), F32)),
            summed=1,
        )
        grad_memory = carry(keep, reach, False)
        grad_query_gate, grad_keys, grad_values = by_slot(
            local_back_kernel,
            (grad_retained, grad_gate, queries, keys, values, memory, columns, lines)
            + (cosine, sine),
            (rate,),
            (0, 1, 2, 3, 4, 5, 6, 7, 10, 8, 9),
            (rows_of_width(KEY + VAL), rows_of_width(KEY, F32), rows_of_width(VAL, F32)),
        )
        (grad_key_value,) = by_slot(
            state_back_kernel,
            (grad_keys, grad_values, keys, values, grad_memory, columns, cosine, sine),
            (),
            range(8),
            (rows_of_width(KEY + VAL),),
        )
        grads = jnp.concatenate(
            [grad_query_gate[..., :KEY], grad_key_value, grad_query_gate[..., KEY:]], axis=-1
        )
    groupscale_grad, groupshift_grad = group_sums[0], group_sums[1]
    grads = grads.reshape(4 * rows, 2 * KEY + 2 * VAL)
    gate_grad = contract_rows(normed, grads[:, 2 * KEY + VAL :]).astype(BF16)
    first_grad = contract_rows(normed, grads[:, : 2 * KEY + VAL]).astype(BF16)
    grads = after(grads, gate_grad, first_grad)
    far_terms = contract_cols(grads[4 * half :], project).astype(BF16)
    far_terms = swap_core(far_terms).astype(F32)
    far_corner = contract_cols(grads[3 * half : 4 * half], project) + far_terms[3 * half :]
    own_terms = contract_cols(grads[: 3 * half], project) + far_terms[: 3 * half]
    own_terms = [own_terms[slot * half : (slot + 1) * half] for slot in range(3)]
    grad_normed = fold(own_terms + [far_corner.astype(BF16)])
    output_grad = scatter(output_grad, 1)
    gate_grad = scatter(gate_grad, 0)
    first_grad = scatter(first_grad, 0)
    prescale_grad = jnp.sum(grad_normed * scaled, axis=0)
    grad_scaled = grad_normed * prescale
    grad_rows = grad_residual + inverse * (
        grad_scaled - scaled * jnp.mean(grad_scaled * scaled, axis=-1, keepdims=True)
    )
    grad_rows, first_grad = lax.optimization_barrier((grad_rows, first_grad))
    first_near = swap_batch(first_grad, 1), swap_batch(first_grad, 2)
    if within:
        parts = send_back(grad_rows.astype(BF16))
        *parts, first, second = lax.optimization_barrier(tuple(parts) + first_near)
        first_near = first, second
        tokens_grad = place_back(parts, F32)
    else:
        tokens_grad = both_rows(grad_rows, swap_core(grad_rows))

    by_width = [prescale_grad, postscale_grad, postshift_grad, outputbias_grad]
    over_cores = swap_core(jnp.concatenate([hiddenbias_grad[part:]] + by_width))
    over_cores = over_cores + jnp.concatenate([hiddenbias_grad[:part]] + by_width)
    spaced = [
        lax.dynamic_update_slice(jnp.zeros((4 * part,), F32), piece, (place * part,))
        for piece in (over_cores[:part], groupscale_grad, groupshift_grad)
    ]
    sums = total(jnp.concatenate([over_cores[part:]] + spaced))
    cuts = [width * at for at in range(1, 5)] + [4 * width + 4 * part, 4 * width + 8 * part]
    prescale_sum, postscale_sum, postshift_sum, outputbias_sum, hiddenbias_sum, scale_sum, shift_sum = (
        jnp.split(sums, cuts)
    )

    def all_pieces(grad):
        return (grad,) + spread(grad)

    reduce_pieces = all_pieces(reduce_grad)
    expand_pieces = all_pieces(expand_grad)
    output_pieces = all_pieces(output_grad)
    gate_pieces = all_pieces(gate_grad)
    first_pieces = (first_grad,) + relay(*first_near)
    return (
        layer_output[None],
        tokens_grad[None],
        prescale_sum,
        place_columns([piece[:, :KEY] for piece in first_pieces], place, KEY),
        place_columns([piece[:, KEY : 2 * KEY] for piece in first_pieces], place, KEY),
        place_columns([piece[:, 2 * KEY :] for piece in first_pieces], place, VAL),
        place_columns(gate_pieces, place, VAL),
        scale_sum,
        shift_sum,
        place_rows(output_pieces, place, VAL),
        postscale_sum,
        postshift_sum,
        place_columns(expand_pieces, place, part),
        hiddenbias_sum,
        place_rows(reduce_pieces, place, part),
        outputbias_sum,
    )


def solution(mesh):
    in_specs = (
        P("batch", "seq", None),
        P(),
        P("seq", "head"),
        P("seq", "head"),
        P("seq", "head"),
        P("seq", "head"),
        P("head"),
        P("head"),
        P("head", "seq"),
        P(),
        P(),
        P("seq", "head"),
        P("head"),
        P("head", "seq"),
        P(),
        P("batch", "seq", None),
        P("batch", None),
        P("batch", "seq"),
    )
    out_specs = (
        P("batch", "seq", None),
        P("batch", "seq", None),
        P(),
        P("seq", "head"),
        P("seq", "head"),
        P("seq", "head"),
        P("seq", "head"),
        P("head"),
        P("head"),
        P("head", "seq"),
        P(),
        P(),
        P("seq", "head"),
        P("head"),
        P("head", "seq"),
        P(),
    )
    return jax.shard_map(body, mesh=mesh, in_specs=in_specs, out_specs=out_specs, check_vma=False)
```

```python
import math

import jax
import jax.numpy as jnp
from jax import lax
from jax.experimental import pallas as pl
from jax.experimental.pallas import tpu as pltpu
from jax.sharding import PartitionSpec as P

KEY = 256
VAL = 512
F32 = jnp.float32
BF16 = jnp.bfloat16


def swap_core(value):
    return lax.ppermute(value, "head", [(0, 1), (1, 0)])


def swap_batch(value, mask):
    return lax.ppermute(value, "batch", [(place, place ^ mask) for place in range(4)])


def after(value, *earlier):
    return lax.optimization_barrier((value,) + earlier)[0]


def spread(piece):
    return relay(swap_batch(piece, 1), swap_batch(piece, 2))


def relay(first, second):
    middle = first.shape[0] // 2
    upper = swap_batch(first[:middle], 2)
    lower = swap_batch(second[middle:], 1)
    return first, second, jnp.concatenate([upper, lower], axis=0)


def fold(parts):
    middle = parts[3].shape[0] // 2
    far = parts[3]
    upper = swap_batch(far[:middle], 1)
    lower = swap_batch(far[middle:], 2)
    to_first = jnp.concatenate(
        [parts[1][:middle], parts[1][middle:] + lower.astype(F32)], axis=0
    ).astype(BF16)
    to_second = jnp.concatenate(
        [parts[2][:middle] + upper.astype(F32), parts[2][middle:]], axis=0
    ).astype(BF16)
    first = swap_batch(to_first, 1)
    second = swap_batch(to_second, 2)
    return parts[0] + first.astype(F32) + second.astype(F32)


def total(value):
    for axis in ("batch", "seq"):
        count = lax.axis_size(axis)
        step = 1
        while step < count:
            moved = lax.ppermute(value, axis, [(place, place ^ step) for place in range(count)])
            value = value + moved
            step *= 2
    return value


def turn(value, steps):
    count = lax.axis_size("seq")
    return lax.ppermute(
        value, "seq", [(source, (source + steps) % count) for source in range(count)]
    )


def hop(value, source, target):
    return lax.ppermute(value, "seq", [(source, target)])


def carry(keep, added, forward):
    count = lax.axis_size("seq")
    entered = []
    for chunk in range(0, 4, 2):
        factor = keep[chunk : chunk + 2, None, None]
        own = added[chunk : chunk + 2]
        state = jnp.zeros(own.shape, BF16)
        for step in range(count - 1):
            sent = (factor * state.astype(F32) + own).astype(BF16)
            source, target = (step, step + 1) if forward else (count - 1 - step, count - 2 - step)
            state = state + hop(sent, source, target)
        entered.append(state)
    return jnp.concatenate(entered, axis=0)


def dot(left, right):
    return jnp.dot(left, right, preferred_element_type=F32)


def contract_rows(left, right):
    return lax.dot_general(left, right, (((0,), (0,)), ((), ())), preferred_element_type=F32)


def contract_cols(left, right):
    return lax.dot_general(left, right, (((1,), (1,)), ((), ())), preferred_element_type=F32)


def normalize_back(grad_unit, unit_norm, inverse):
    mean_grad = jnp.mean(grad_unit, axis=-1, keepdims=True)
    mean_cross = jnp.mean(grad_unit * unit_norm, axis=-1, keepdims=True)
    return inverse * (grad_unit - mean_grad - unit_norm * mean_cross)


def rotated(values, cosine, sine):
    middle = values.shape[-1] // 2
    former, latter = (values[:, :middle], values[:, middle:])
    return jnp.concatenate(
        [former * cosine - latter * sine, latter * cosine + former * sine], axis=-1
    )


def flat(ref):
    value = ref[...]
    return value.reshape(-1, value.shape[-1])


def put(ref, value):
    ref[...] = value.reshape(ref.shape).astype(ref.dtype)


def weigh(value, weight):
    return (value.astype(F32) * weight).astype(BF16)


def decay_of(columns, lines, rate):
    distance = columns[:, 3:4] - lines[1:2]
    linked = (columns[:, 2:3] == lines[0:1]) & (distance >= 0)
    return jnp.where(linked, jnp.exp(jnp.maximum(distance, 0.0) * rate), 0.0)


def key_value_kernel(normed, weight, cosine, sine, columns, keys, values, added):
    product = dot(flat(normed), weight[...])
    key = (rotated(product[:, :KEY], flat(cosine), flat(sine)) * KEY ** (-0.5)).astype(BF16)
    value = product[:, KEY:].astype(BF16)
    put(keys, key)
    put(values, value)
    put(added, contract_rows(weigh(key, flat(columns)[:, 1:2]), value))


def retain_kernel(
    normed, weight, cosine, sine, columns, lines, rate, keys, values, memory, scale, shift,
    queries, gate, unit, inverse, gated,
):
    product = dot(flat(normed), weight[...])
    query = rotated(product[:, :KEY], flat(cosine), flat(sine)).astype(BF16)
    table = flat(columns)
    decay = decay_of(table, flat(lines), rate[...])
    mixing = (contract_cols(query, flat(keys)) * decay).astype(BF16)
    retained = dot(mixing, flat(values)) + dot(weigh(query, table[:, 0:1]), flat(memory))
    centred = retained - jnp.mean(retained, axis=-1, keepdims=True)
    factor = lax.rsqrt(jnp.mean(centred * centred, axis=-1, keepdims=True) + 1.0)
    unit_norm = centred * factor
    gate_pre = product[:, KEY:]
    put(queries, query)
    put(gate, gate_pre)
    put(unit, unit_norm)
    put(inverse, factor)
    grouped = unit_norm * scale[...] + shift[...]
    put(gated, gate_pre * jax.nn.sigmoid(gate_pre) * grouped)


def gate_back_kernel(
    grad_own, grad_far, gate, unit, inverse, scale, shift, columns, queries,
    grad_gate, grad_retained, reach, sums,
):
    grad_gated = jnp.concatenate([flat(grad_own), flat(grad_far)], axis=0).astype(F32)
    gate_pre, unit_norm = flat(gate), flat(unit)
    grouped = unit_norm * scale[...] + shift[...]
    sigmoid = jax.nn.sigmoid(gate_pre)
    put(grad_gate, grad_gated * grouped * sigmoid * (1.0 + gate_pre * (1.0 - sigmoid)))
    grad_grouped = grad_gated * (gate_pre * sigmoid)
    part = jnp.concatenate(
        [
            jnp.sum(grad_grouped * unit_norm, axis=0, keepdims=True),
            jnp.sum(grad_grouped, axis=0, keepdims=True),
        ],
        axis=0,
    )

    @pl.when(pl.program_id(0) == 0)
    def first():
        sums[...] = part

    @pl.when(pl.program_id(0) > 0)
    def later():
        sums[...] += part

    grad = normalize_back(grad_grouped * scale[...], unit_norm, flat(inverse)).astype(BF16)
    put(grad_retained, grad)
    put(reach, contract_rows(weigh(flat(queries), flat(columns)[:, 0:1]), grad))


def local_back_kernel(
    grad_retained, grad_gate, queries, keys, values, memory, columns, lines, rate, cosine, sine,
    grad_query_gate, grad_keys, grad_values,
):
    grad, query, key, value = flat(grad_retained), flat(queries), flat(keys), flat(values)
    table = flat(columns)
    decay = decay_of(table, flat(lines), rate[...])
    mixing = (contract_cols(query, key) * decay).astype(BF16)
    grad_scores = (contract_cols(grad, value) * decay).astype(BF16)
    grad_query = dot(grad_scores, key) + table[:, 0:1] * contract_cols(grad, flat(memory))
    grad_query = rotated(grad_query, flat(cosine), -flat(sine)).astype(BF16)
    put(grad_query_gate, jnp.concatenate([grad_query, flat(grad_gate)], axis=-1))
    put(grad_keys, contract_rows(grad_scores, query))
    put(grad_values, contract_rows(mixing, grad))


def state_back_kernel(
    grad_keys, grad_values, keys, values, grad_memory, columns, cosine, sine, grad_key_value
):
    weight = flat(columns)[:, 1:2]
    state = flat(grad_memory)
    grad_key = flat(grad_keys) + weight * contract_cols(flat(values), state)
    grad_key = rotated(grad_key, flat(cosine), -flat(sine)) * KEY ** (-0.5)
    grad_value = flat(grad_values) + dot(weigh(flat(keys), weight), state)
    put(
        grad_key_value,
        jnp.concatenate([grad_key.astype(BF16), grad_value.astype(BF16)], axis=-1),
    )


def stream_kernel(
    normed, weight, cosine, sine, columns, lines, rate, scale, shift,
    queries, keys, values, memory, gate, unit, inverse, gated, state,
):
    @pl.when(pl.program_id(0) == 0)
    def first():
        state[...] = jnp.zeros_like(state)

    product = dot(flat(normed), weight[...])
    table = flat(columns)
    query = rotated(product[:, :KEY], flat(cosine), flat(sine)).astype(BF16)
    key = rotated(product[:, KEY : 2 * KEY], flat(cosine), flat(sine)) * KEY ** (-0.5)
    key = key.astype(BF16)
    value = product[:, 2 * KEY : 2 * KEY + VAL].astype(BF16)
    gate_pre = product[:, 2 * KEY + VAL :]
    low = state[...].astype(BF16)
    decay = decay_of(table, flat(lines), rate[...])
    mixing = (contract_cols(query, key) * decay).astype(BF16)
    retained = dot(mixing, value) + dot(weigh(query, table[:, 0:1]), low)
    state[...] = table[0:1, 4:5] * state[...] + contract_rows(weigh(key, table[:, 1:2]), value)
    centred = retained - jnp.mean(retained, axis=-1, keepdims=True)
    factor = lax.rsqrt(jnp.mean(centred * centred, axis=-1, keepdims=True) + 1.0)
    unit_norm = centred * factor
    put(queries, query)
    put(keys, key)
    put(values, value)
    put(memory, low)
    put(gate, gate_pre)
    put(unit, unit_norm)
    put(inverse, factor)
    grouped = unit_norm * scale[...] + shift[...]
    put(gated, gate_pre * jax.nn.sigmoid(gate_pre) * grouped)


def stream_back_kernel(
    grad_own, grad_far, gate, unit, inverse, scale, shift, columns, lines, rate, cosine, sine,
    queries, keys, values, memory, grads, sums, state,
):
    grad_gated = jnp.concatenate([flat(grad_own), flat(grad_far)], axis=0).astype(F32)
    gate_pre, unit_norm, table = flat(gate), flat(unit), flat(columns)
    query, key, value = flat(queries), flat(keys), flat(values)
    entry, weight = table[:, 0:1], table[:, 1:2]
    grouped = unit_norm * scale[...] + shift[...]
    sigmoid = jax.nn.sigmoid(gate_pre)
    grad_gate = grad_gated * grouped * sigmoid * (1.0 + gate_pre * (1.0 - sigmoid))
    grad_grouped = grad_gated * (gate_pre * sigmoid)

    @pl.when(pl.program_id(0) == 0)
    def first():
        state[...] = jnp.zeros_like(state)
        sums[...] = jnp.zeros_like(sums)

    sums[0:1] += jnp.sum(grad_grouped * unit_norm, axis=0, keepdims=True)
    sums[1:2] += jnp.sum(grad_grouped, axis=0, keepdims=True)
    grad = normalize_back(grad_grouped * scale[...], unit_norm, flat(inverse)).astype(BF16)
    decay = decay_of(table, flat(lines), rate[...])
    mixing = (contract_cols(query, key) * decay).astype(BF16)
    grad_scores = (contract_cols(grad, value) * decay).astype(BF16)
    low = state[...].astype(BF16)
    grad_query = dot(grad_scores, key) + entry * contract_cols(grad, flat(memory))
    grad_key = contract_rows(grad_scores, query) + weight * contract_cols(value, low)
    grad_value = contract_rows(mixing, grad) + dot(weigh(key, weight), low)
    state[...] = table[0:1, 4:5] * state[...] + contract_rows(weigh(query, entry), grad)
    cosines, sines = flat(cosine), -flat(sine)
    put(
        grads,
        jnp.concatenate(
            [
                rotated(grad_query, cosines, sines).astype(BF16),
                (rotated(grad_key, cosines, sines) * KEY ** (-0.5)).astype(BF16),
                grad_value.astype(BF16),
                grad_gate.astype(BF16),
            ],
            axis=-1,
        ),
    )


def rows_spec(value, whole=False):
    if whole:
        return pl.BlockSpec(value.shape, lambda slot: (0,) * len(value.shape))
    if len(value.shape) == 4:
        two, _, half, width = value.shape
        return pl.BlockSpec((two, 1, half, width), lambda slot: (0, slot, 0, 0))
    return pl.BlockSpec((1,) + value.shape[1:], lambda slot: (slot, 0, 0))


def block_spec(value, whole=False, last=False):
    if whole:
        return pl.BlockSpec(value.shape, lambda step: (0,) * len(value.shape))
    rank = len(value.shape)
    shape = value.shape[: rank - 3] + (1,) + value.shape[rank - 2 :]
    return pl.BlockSpec(
        shape, lambda step: (0,) * (rank - 3) + (3 - step if last else step,) + (0, 0)
    )


def by_block(kernel, inputs, shared, out_shapes, last, summed=0):
    outs = [jax.ShapeDtypeStruct(shape, dtype) for shape, dtype in out_shapes]
    return pl.pallas_call(
        kernel,
        grid=(4,),
        in_specs=[block_spec(v, at in shared, last) for at, v in enumerate(inputs)],
        out_specs=[block_spec(v, at >= len(outs) - summed, last) for at, v in enumerate(outs)],
        out_shape=outs,
        scratch_shapes=[pltpu.VMEM((KEY, VAL), F32)],
        compiler_params=pltpu.CompilerParams(
            dimension_semantics=("arbitrary",), vmem_limit_bytes=56 * 2**20
        ),
    )(*inputs)


def by_slot(kernel, slotted, shared, order, out_shapes, summed=0):
    inputs = tuple(slotted) + tuple(shared)
    specs = [rows_spec(v) for v in slotted] + [rows_spec(v, True) for v in shared]
    outs = [jax.ShapeDtypeStruct(shape, dtype) for shape, dtype in out_shapes]
    out_specs = [rows_spec(v, at >= len(outs) - summed) for at, v in enumerate(outs)]
    return pl.pallas_call(
        kernel,
        grid=(4,),
        in_specs=[specs[at] for at in order],
        out_specs=out_specs,
        out_shape=outs,
        compiler_params=pltpu.CompilerParams(
            dimension_semantics=("arbitrary",), vmem_limit_bytes=56 * 2**20
        ),
    )(*[inputs[at] for at in order])


def slot_products(product, left, right):
    size = left.shape[0] // 4
    far = product(left[3 * size :], right).astype(BF16)
    left, right, far = lax.optimization_barrier((left, right, far))
    near = product(left[size : 3 * size], right)
    own = product(left[:size], right)
    return [own, near[:size], near[size:], far]


def place_columns(pieces, place, width):
    rows = pieces[0].shape[0]
    result = jnp.zeros((rows, 4 * width), F32)
    for slot, piece in enumerate(pieces):
        result = lax.dynamic_update_slice(result, piece.astype(F32), (0, (place ^ slot) * width))
    return result


def place_rows(pieces, place, height):
    result = jnp.zeros((4 * height, pieces[0].shape[1]), F32)
    for slot, piece in enumerate(pieces):
        result = lax.dynamic_update_slice(result, piece.astype(F32), ((place ^ slot) * height, 0))
    return result


def body(
    tokens,
    prescale,
    query_weight,
    key_weight,
    value_weight,
    gate_weight,
    groupscale,
    groupshift,
    output_weight,
    postscale,
    postshift,
    expand_weight,
    hiddenbias,
    reduce_weight,
    outputbias,
    cotangent,
    doc_lengths,
    segments,
):
    _, rows, width = tokens.shape
    half = rows // 2
    part = hiddenbias.shape[0] // 4
    core = lax.axis_index("head")
    place = lax.axis_index("batch")
    block = lax.axis_index("seq")
    within = lax.axis_size("seq") == 4
    size = half // 4

    def shares_of(*values):
        def share(of):
            cut = [lax.dynamic_slice_in_dim(v, (2 * of + core) * size, size, 0) for v in values]
            return jnp.concatenate(cut + [marks], axis=0)

        held = [share(place)]
        held += [swap_batch(share(place ^ slot), slot) for slot in (1, 2, 3)]
        return jnp.stack(held)

    def plane_of(held):
        result = jnp.zeros(held.shape, held.dtype)
        for steps in range(4):
            moved = lax.dynamic_index_in_dim(held, place ^ ((block + steps) % 4), 0, True)
            if steps:
                moved = turn(moved, steps)
            result = lax.dynamic_update_slice_in_dim(result, moved, (block - steps) % 4, 0)
        return result

    def send_back(value):
        value = value.reshape(4, size, width)
        parts = [
            lax.dynamic_index_in_dim(value, (block - steps) % 4, 0, True) for steps in range(4)
        ]
        return parts[:1] + [turn(parts[steps], -steps) for steps in (1, 2, 3)]

    def place_back(parts, dtype):
        held = jnp.zeros((4, size, width), parts[0].dtype)
        for steps, part in enumerate(parts):
            held = lax.dynamic_update_slice_in_dim(held, part, (block + steps) % 4, 0)
        own = []
        for slot in range(4):
            moved = lax.dynamic_index_in_dim(held, place ^ slot, 0, False)
            own.append(swap_batch(moved, slot) if slot else moved)
        own = jnp.stack(own)
        far = swap_core(own)
        result = jnp.zeros((8, size, width), dtype)
        for slot in range(4):
            for side, shared in ((core, own), (1 - core, far)):
                result = lax.dynamic_update_slice_in_dim(
                    result, shared[slot : slot + 1].astype(dtype), 2 * (place ^ slot) + side, 0
                )
        return result.reshape(rows, width)

    def both_rows(own, far):
        result = jnp.zeros((rows, width), own.dtype)
        result = lax.dynamic_update_slice_in_dim(result, own, core * half, 0)
        return lax.dynamic_update_slice_in_dim(result, far, (1 - core) * half, 0)

    def cols_of(weight, size):
        return lax.dynamic_slice_in_dim(weight, place * size, size, 1)

    def rows_of(weight, size):
        return lax.dynamic_slice_in_dim(weight, place * size, size, 0)

    def gather_rows(weight):
        return lax.all_gather(weight, "seq", axis=0, tiled=True)

    def gather_cols(weight):
        return lax.all_gather(weight, "seq", axis=1, tiled=True)

    def scatter(grad, dimension):
        return lax.psum_scatter(grad.astype(BF16), "seq", scatter_dimension=dimension, tiled=True)

    project = jnp.concatenate(
        [
            cols_of(query_weight, KEY),
            cols_of(key_weight, KEY),
            cols_of(value_weight, VAL),
            cols_of(gate_weight, VAL),
        ],
        axis=1,
    )
    tokens = after(tokens, project)
    project = gather_rows(project)

    steps = jnp.arange(half, dtype=jnp.int32)
    if within:
        lengths = doc_lengths[0]
        marks = jnp.concatenate([segments[0], lengths // 64, lengths % 64]).astype(BF16)
        marks = jnp.pad(marks[None], ((0, 7), (0, width - marks.shape[0])))
        held = shares_of(cotangent[0], tokens[0])
        held_dy, held = held[:, :size], held[:, size:]
        held = plane_of(held)
        tokens_own = held[:, :size].reshape(half, width)
        marks = held[:, size].astype(jnp.int32)
        natural = marks[:, :rows]
        count = doc_lengths.shape[1]
        spans = marks[:, rows : rows + count] * 64 + marks[:, rows + count : rows + 2 * count]
        before = jnp.concatenate([jnp.full((1,), -1, jnp.int32), natural[:-1, rows - 1]])
        side, slot = jnp.arange(2)[:, None], jnp.arange(4)[None]
        share = 2 * (place ^ slot) + (core ^ side)
        index = share[:, :, None, None] * size + steps[:size]
        segment = jnp.take(natural.reshape(4, 8, size), share.reshape(8), axis=1)
        segment = segment.transpose(1, 0, 2).reshape(2, 4, 4, size)
        index = jnp.broadcast_to(index, segment.shape)
        at_block = jnp.arange(4)[None, None, :, None]
        stream_index = at_block * rows + index
        form = (1, 1, 4, 1)
    else:
        before = lax.ppermute(
            segments[0, rows - 1 :],
            "seq",
            [(source, source + 1) for source in range(lax.axis_size("seq") - 1)],
        )
        before = jnp.where(block == 0, -1, before)
        marks = jnp.concatenate([segments[0], doc_lengths[0], before])[None]
        marks = jnp.concatenate([marks, swap_batch(marks, 1)], axis=0)
        marks = jnp.concatenate([marks, swap_batch(marks, 2)], axis=0)
        natural, spans, before = marks[:, :rows], marks[:, rows:-1], marks[:, -1]
        tokens_own = lax.dynamic_slice_in_dim(tokens[0], core * half, half, 0)
        dy_own = lax.dynamic_slice_in_dim(cotangent[0], core * half, half, 0)
        index = jnp.stack([core * half + steps, (1 - core) * half + steps])[:, None]
        upper, lower = natural[None, :, :half], natural[None, :, half:]
        segment = jnp.where(
            core == 0,
            jnp.concatenate([upper, lower], axis=0),
            jnp.concatenate([lower, upper], axis=0),
        )
        index = jnp.broadcast_to(index, segment.shape)
        stream_index = block * rows + index
        form = (1, 4, 1)
    wide = tokens_own.astype(F32)
    inverse = lax.rsqrt(jnp.mean(wide * wide, axis=-1, keepdims=True) + 1e-06)
    scaled = wide * inverse
    normed_own = lax.optimization_barrier((scaled * prescale).astype(BF16))
    arrived = spread(normed_own)
    if within:
        dy_own = plane_of(after(held_dy, arrived[0])).reshape(half, width)
    normed = (normed_own,) + arrived
    normed = jnp.concatenate(normed + tuple(swap_core(piece) for piece in normed), axis=0)
    normed = lax.optimization_barrier(normed)
    dy_rows = jnp.concatenate((dy_own,) + spread(after(dy_own, arrived)), axis=0)
    output_own = gather_cols(after(rows_of(output_weight, VAL), arrived))
    expand_own = gather_rows(after(cols_of(expand_weight, part), normed))
    reduce_own = gather_cols(after(rows_of(reduce_weight, part), normed))

    last = natural[:, rows - 1]
    ends = jnp.cumsum(spans, axis=1).reshape(form + (-1,))
    spans = spans.reshape(form + (-1,))
    starts = jnp.sum(jnp.where(ends <= stream_index[..., None], spans, 0), axis=-1)
    positions = (stream_index - starts).astype(F32)
    middle = KEY // 2
    frequency = jnp.exp(-math.log(10000.0) * jnp.arange(middle, dtype=F32) / (middle - 1))
    phases = positions[..., None] * frequency
    cosine, sine = jnp.cos(phases), jnp.sin(phases)
    head = (core * 4 + place).astype(F32)
    log_rate = jnp.log1p(-jnp.exp2(-5.0 - head))
    entry = jnp.exp((index + 1).astype(F32) * log_rate) * (
        segment == before.reshape(form)
    ).astype(F32)
    exit_weight = jnp.exp((rows - 1 - index).astype(F32) * log_rate) * (
        segment == last.reshape(form)
    ).astype(F32)
    keep = jnp.exp(rows * log_rate) * (last == before).astype(F32)
    segment, index = segment.astype(F32), index.astype(F32)
    wide_keep = jnp.broadcast_to(keep.reshape(form), segment.shape)
    columns = jnp.stack([entry, exit_weight, segment, index, wide_keep], axis=-1)
    lines = jnp.stack([segment, index], axis=0)
    if within:
        lines = lines.transpose(3, 0, 1, 2, 4)
    else:
        lines = lines.transpose(2, 0, 1, 3)
    lines = lines.reshape(4, 2, rows)
    rate = jnp.full((1, 1), log_rate)
    cosine, sine, columns, lines = lax.optimization_barrier((cosine, sine, columns, lines))

    def rows_of_width(size, dtype=BF16):
        return (segment.shape + (size,), dtype)

    def entries(size, dtype=BF16):
        return ((4, KEY, size), dtype)

    scale_own = lax.dynamic_slice_in_dim(groupscale, place * VAL, VAL, 0)[None]
    shift_own = lax.dynamic_slice_in_dim(groupshift, place * VAL, VAL, 0)[None]
    normed_slots = normed.reshape(segment.shape + (width,))
    if within:
        queries, keys, values, memory, gate, unit, group_inverse, gated = by_block(
            stream_kernel,
            (normed_slots, project, cosine, sine, columns, lines, rate, scale_own, shift_own),
            (1, 6, 7, 8),
            (
                rows_of_width(KEY),
                rows_of_width(KEY),
                rows_of_width(VAL),
                entries(VAL),
                rows_of_width(VAL, F32),
                rows_of_width(VAL, F32),
                rows_of_width(1, F32),
                rows_of_width(VAL),
            ),
            False,
        )
    else:
        key_value = project[:, KEY : 2 * KEY + VAL]
        query_gate = jnp.concatenate([project[:, :KEY], project[:, 2 * KEY + VAL :]], axis=1)
        keys, values, added = by_slot(
            key_value_kernel,
            (normed_slots, cosine, sine, columns),
            (key_value,),
            (0, 4, 1, 2, 3),
            (rows_of_width(KEY), rows_of_width(VAL), entries(VAL, F32)),
        )
        memory = carry(keep, added, True)
        queries, gate, unit, group_inverse, gated = by_slot(
            retain_kernel,
            (normed_slots, cosine, sine, columns, lines, keys, values, memory),
            (query_gate, rate, scale_own, shift_own),
            (0, 8, 1, 2, 3, 4, 9, 5, 6, 7, 10, 11),
            (
                rows_of_width(KEY),
                rows_of_width(VAL, F32),
                rows_of_width(VAL, F32),
                rows_of_width(1, F32),
                rows_of_width(VAL),
            ),
        )
    gated_own = gated[0].reshape(4 * half, VAL)
    gated_far = swap_core(gated[1].reshape(4 * half, VAL))
    gated_both = jnp.concatenate([gated_own, gated_far], axis=-1)

    output_own = after(output_own, gated_both)
    output_both = jnp.concatenate([output_own, swap_core(output_own)], axis=0)
    bias_own = lax.dynamic_slice_in_dim(hiddenbias, place * part, part, 0)
    bias_both = jnp.concatenate([bias_own, swap_core(bias_own)], axis=0)

    branch = fold(slot_products(dot, gated_both, output_both))
    residual = wide + branch
    shifted = residual - jnp.mean(residual, axis=-1, keepdims=True)
    layer_inverse = lax.rsqrt(jnp.mean(shifted * shifted, axis=-1, keepdims=True) + 1e-05)
    standard = shifted * layer_inverse
    layered_own = (standard * postscale + postshift).astype(BF16)
    layered = jnp.concatenate((layered_own,) + spread(layered_own), axis=0)
    expand_own = after(expand_own, layered_own)
    expand_both = jnp.concatenate([expand_own, swap_core(expand_own)], axis=1)
    reduce_own = after(reduce_own, expand_own)
    reduce_both = jnp.concatenate([reduce_own, swap_core(reduce_own)], axis=0)

    hidden = dot(layered, expand_both) + bias_both
    cumulative = 0.5 * (1.0 + lax.erf(hidden * 0.5**0.5))
    active = (hidden * cumulative).astype(BF16)
    def core_sum(grad, dimension):
        size = grad.shape[dimension] // 2
        own = lax.slice_in_dim(grad, 0, size, axis=dimension)
        far = lax.slice_in_dim(grad, size, 2 * size, axis=dimension)
        return own + swap_core(far.astype(BF16)).astype(F32)

    dy_wide = dy_own.astype(F32)
    outputbias_grad = jnp.sum(dy_wide, axis=0)
    reduce_grad = scatter(core_sum(contract_rows(active, dy_rows), 0), 1)
    grad_active = contract_cols(dy_rows, reduce_both)
    slope = cumulative + hidden * jnp.exp(-0.5 * hidden * hidden) * (0.5 / math.pi) ** 0.5
    grad_hidden = (grad_active * slope).astype(BF16)
    hiddenbias_grad = jnp.sum(grad_hidden.astype(F32), axis=0)
    grad_layered = fold(slot_products(contract_cols, grad_hidden, expand_both))
    expand_grad = scatter(core_sum(contract_rows(layered, grad_hidden), 1), 0)
    postscale_grad = jnp.sum(grad_layered * standard, axis=0)
    postshift_grad = jnp.sum(grad_layered, axis=0)
    grad_residual = dy_wide + normalize_back(grad_layered * postscale, standard, layer_inverse)
    grad_branch_own = grad_residual.astype(BF16)
    grad_branch = jnp.concatenate((grad_branch_own,) + spread(grad_branch_own), axis=0)

    expanded = fold(slot_products(dot, after(active, grad_branch), reduce_both))
    output_rows = (residual + expanded + outputbias).astype(BF16)
    if within:
        layer_output = place_back(send_back(output_rows), BF16)
    else:
        layer_output = both_rows(output_rows, swap_core(output_rows))

    grad_gated_both = contract_cols(grad_branch, output_both).astype(BF16)
    grad_gated_own = grad_gated_both[:, :VAL].reshape(segment.shape[1:] + (VAL,))
    grad_gated_far = swap_core(grad_gated_both[:, VAL:]).reshape(segment.shape[1:] + (VAL,))
    output_grad = core_sum(contract_rows(gated_both, grad_branch), 0)
    if within:
        grads, group_sums = by_block(
            stream_back_kernel,
            (grad_gated_own, grad_gated_far, gate, unit, group_inverse, scale_own, shift_own)
            + (columns, lines, rate, cosine, sine, queries, keys, values, memory),
            (5, 6, 9),
            (rows_of_width(2 * KEY + 2 * VAL), ((2, VAL), F32)),
            True,
            summed=1,
        )
    else:
        grad_gate, grad_retained, reach, group_sums = by_slot(
            gate_back_kernel,
            (grad_gated_own, grad_gated_far, gate, unit, group_inverse, columns, queries),
            (scale_own, shift_own),
            (0, 1, 2, 3, 4, 7, 8, 5, 6),
            (rows_of_width(VAL), rows_of_width(VAL), entries(VAL, F32), ((2, VAL), F32)),
            summed=1,
        )
        grad_memory = carry(keep, reach, False)
        grad_query_gate, grad_keys, grad_values = by_slot(
            local_back_kernel,
            (grad_retained, grad_gate, queries, keys, values, memory, columns, lines)
            + (cosine, sine),
            (rate,),
            (0, 1, 2, 3, 4, 5, 6, 7, 10, 8, 9),
            (rows_of_width(KEY + VAL), rows_of_width(KEY, F32), rows_of_width(VAL, F32)),
        )
        (grad_key_value,) = by_slot(
            state_back_kernel,
            (grad_keys, grad_values, keys, values, grad_memory, columns, cosine, sine),
            (),
            range(8),
            (rows_of_width(KEY + VAL),),
        )
        grads = jnp.concatenate(
            [grad_query_gate[..., :KEY], grad_key_value, grad_query_gate[..., KEY:]], axis=-1
        )
    groupscale_grad, groupshift_grad = group_sums[0], group_sums[1]
    grads = grads.reshape(4 * rows, 2 * KEY + 2 * VAL)
    gate_grad = contract_rows(normed, grads[:, 2 * KEY + VAL :]).astype(BF16)
    first_grad = contract_rows(normed, grads[:, : 2 * KEY + VAL]).astype(BF16)
    grads = after(grads, gate_grad, first_grad)
    far_terms = contract_cols(grads[4 * half :], project).astype(BF16)
    far_terms = swap_core(far_terms).astype(F32)
    far_corner = contract_cols(grads[3 * half : 4 * half], project) + far_terms[3 * half :]
    own_terms = contract_cols(grads[: 3 * half], project) + far_terms[: 3 * half]
    own_terms = [own_terms[slot * half : (slot + 1) * half] for slot in range(3)]
    grad_normed = fold(own_terms + [far_corner.astype(BF16)])
    output_grad = scatter(output_grad, 1)
    gate_grad = scatter(gate_grad, 0)
    first_grad = scatter(first_grad, 0)
    prescale_grad = jnp.sum(grad_normed * scaled, axis=0)
    grad_scaled = grad_normed * prescale
    grad_rows = grad_residual + inverse * (
        grad_scaled - scaled * jnp.mean(grad_scaled * scaled, axis=-1, keepdims=True)
    )
    grad_rows, first_grad = lax.optimization_barrier((grad_rows, first_grad))
    first_near = swap_batch(first_grad, 1), swap_batch(first_grad, 2)
    if within:
        parts = send_back(grad_rows.astype(BF16))
        *parts, first, second = lax.optimization_barrier(tuple(parts) + first_near)
        first_near = first, second
        tokens_grad = place_back(parts, F32)
    else:
        tokens_grad = both_rows(grad_rows, swap_core(grad_rows))

    by_width = [prescale_grad, postscale_grad, postshift_grad, outputbias_grad]
    over_cores = swap_core(jnp.concatenate([hiddenbias_grad[part:]] + by_width))
    over_cores = over_cores + jnp.concatenate([hiddenbias_grad[:part]] + by_width)
    spaced = [
        lax.dynamic_update_slice(jnp.zeros((4 * part,), F32), piece, (place * part,))
        for piece in (over_cores[:part], groupscale_grad, groupshift_grad)
    ]
    sums = jnp.concatenate([over_cores[part:]] + spaced)
    sums = total(after(sums, *first_near))
    cuts = [width * at for at in range(1, 5)] + [4 * width + 4 * part, 4 * width + 8 * part]
    prescale_sum, postscale_sum, postshift_sum, outputbias_sum, hiddenbias_sum, scale_sum, shift_sum = (
        jnp.split(sums, cuts)
    )

    def all_pieces(grad):
        return (grad,) + spread(grad)

    reduce_pieces = all_pieces(reduce_grad)
    expand_pieces = all_pieces(expand_grad)
    output_pieces = all_pieces(output_grad)
    gate_pieces = all_pieces(gate_grad)
    first_pieces = (first_grad,) + relay(*first_near)
    return (
        layer_output[None],
        tokens_grad[None],
        prescale_sum,
        place_columns([piece[:, :KEY] for piece in first_pieces], place, KEY),
        place_columns([piece[:, KEY : 2 * KEY] for piece in first_pieces], place, KEY),
        place_columns([piece[:, 2 * KEY :] for piece in first_pieces], place, VAL),
        place_columns(gate_pieces, place, VAL),
        scale_sum,
        shift_sum,
        place_rows(output_pieces, place, VAL),
        postscale_sum,
        postshift_sum,
        place_columns(expand_pieces, place, part),
        hiddenbias_sum,
        place_rows(reduce_pieces, place, part),
        outputbias_sum,
    )


def solution(mesh):
    in_specs = (
        P("batch", "seq", None),
        P(),
        P("seq", "head"),
        P("seq", "head"),
        P("seq", "head"),
        P("seq", "head"),
        P("head"),
        P("head"),
        P("head", "seq"),
        P(),
        P(),
        P("seq", "head"),
        P("head"),
        P("head", "seq"),
        P(),
        P("batch", "seq", None),
        P("batch", None),
        P("batch", "seq"),
    )
    out_specs = (
        P("batch", "seq", None),
        P("batch", "seq", None),
        P(),
        P("seq", "head"),
        P("seq", "head"),
        P("seq", "head"),
        P("seq", "head"),
        P("head"),
        P("head"),
        P("head", "seq"),
        P(),
        P(),
        P("seq", "head"),
        P("head"),
        P("head", "seq"),
        P(),
    )
    return jax.shard_map(body, mesh=mesh, in_specs=in_specs, out_specs=out_specs, check_vma=False)
```
